256 devices in a mesh: slab: 8 (over x, core), pos: 32 (over y, z).
Axes of the slice: x: 4, y: 4, z: 8, core: 2. Of those that a mesh axis runs over, the one named last changes fastest.
Arguments:
- object_field: float32 [2, 8, 4096, 2048], P(None, 'slab', 'pos'), may hold values from -0.25 to 1.15, as said below
- probe_wave: float32 [2, 128, 128], replicated, may hold values from -4.2 to 4.2
- scan_coords: int32 [96, 2], P('pos'), may hold values from 0 to 3968, as said below
- scan_counts: int32 [32], P('pos'), may hold values from 1 to 3, as said below
- measured: float32 [96, 128, 128], P('pos'), may hold values from 0.1 to 3
Outputs:
- object_gradient: float32 [2, 8, 4096, 2048], P(None, 'slab', 'pos')
The draws below stay inside these ranges and needn't reach their ends.
Inputs may be any that keep to these rules, and one draw needn't show every extreme that they name: `object_field`: real parts between 0.85 and 1.15, imaginary parts between -0.25 and 0.25. `scan_coords`: slot q belongs to owner j = q div 3; its row corner lies in [j * 128, (j + 1) * 128) and is at most 3968; its column corner is at most 1920. The first scan_counts[j] slots of owner j are live, the others are not; some owner has all 3 live.
All inputs are finite; a program needn't handle non-finite values.
Results may differ from the reference program's by a relative error of at most 0.02.
Values may be sent and summed in bfloat16 or wider, within the bound.
A program may use at most 64 MiB of HBM per device.

```python
import math
import jax
import jax.numpy as jnp
from jax import lax

P_SIZE = 128
NCOL = 2048
ROWS_DEV = 128
SL_DEV = 1
CAP = 3
SLICES = 8
NOBJ = 4096
SLOTS = 96
N_POS = 32


def draw_object_field(key, part):
    real_part = jax.random.uniform(jax.random.fold_in(key, 31), (SLICES, NOBJ, NCOL), jnp.float32, 0.85, 1.15)
    imag_part = jax.random.uniform(jax.random.fold_in(key, 32), (SLICES, NOBJ, NCOL), jnp.float32, -0.25, 0.25)
    return jnp.stack([real_part, imag_part]).astype(jnp.float32)


def draw_scan_coords(key, part):
    slot_ids = jnp.arange(SLOTS, dtype=jnp.int32)
    owner_ids = slot_ids // CAP
    offsets = jax.random.randint(jax.random.fold_in(key, 11), (SLOTS,), 0, ROWS_DEV, dtype=jnp.int32)
    corner_rows = jnp.minimum(owner_ids * ROWS_DEV + offsets, NOBJ - P_SIZE)
    corner_cols = jax.random.randint(jax.random.fold_in(key, 12), (SLOTS,), 0, NCOL - P_SIZE + 1, dtype=jnp.int32)
    corner_rows = jnp.where(slot_ids == 0, 0, corner_rows)
    corner_cols = jnp.where(slot_ids == 0, 0, corner_cols)
    corner_cols = jnp.where(slot_ids == 1, NCOL - P_SIZE, corner_cols)
    return jnp.stack([corner_rows, corner_cols], axis=1).astype(jnp.int32)


def draw_scan_counts(key, part):
    base_counts = jax.random.randint(jax.random.fold_in(key, 21), (N_POS,), 1, CAP + 1, dtype=jnp.int32)
    chosen = jax.random.randint(jax.random.fold_in(key, 22), (), 0, N_POS, dtype=jnp.int32)
    owner_ids = jnp.arange(N_POS, dtype=jnp.int32)
    return jnp.where(owner_ids == chosen, CAP, base_counts).astype(jnp.int32)


def level_of(own_key, dims, shards, smallest, high):
    factor_of = 1.0
    for axis_at, parts in shards:
        steps = jax.random.uniform(jax.random.fold_in(jax.random.fold_in(own_key, 6), axis_at), (parts,), jnp.float32, smallest / len(shards), high / len(shards))
        factor_of = factor_of * jnp.repeat(jnp.exp(steps), dims[axis_at] // parts).reshape((-1,) + (1,) * (len(dims) - 1 - axis_at))
    return factor_of


def normal_values(rng, dims, deviation, most, kind=jnp.bfloat16):
    entries = jax.random.normal(rng, dims, jnp.float32) * deviation
    return jnp.minimum(jnp.maximum(entries, -most), most).astype(kind)


def setup_inputs(seed: int = 0) -> dict:
    key_list = jax.random.split(jax.random.key(seed), 6)
    return {
        "object_field": draw_object_field(jax.random.fold_in(key_list[5], 71), 0),
        "probe_wave": normal_values(key_list[1], (2, P_SIZE, P_SIZE), 0.7, 4.2, jnp.float32),
        "scan_coords": draw_scan_coords(jax.random.fold_in(key_list[5], 71), 0),
        "scan_counts": draw_scan_counts(jax.random.fold_in(key_list[5], 71), 0),
        "measured": jnp.clip(jnp.exp(math.log(3.0) - 3.4011974 * jax.random.uniform(key_list[4], (SLOTS, P_SIZE, P_SIZE), jnp.float32) ** level_of(key_list[4], (SLOTS, P_SIZE, P_SIZE), ((0, 32),), -0.2, 0.2)), 0.1, 3.0),
    }


spread_factor = 0.5

def fourier_tables(length):
    grid_index = jnp.arange(length, dtype=jnp.int32)
    phase_index = grid_index[:, None] * grid_index[None, :] % length
    angles = phase_index.astype(jnp.float32) * (2.0 * math.pi / length)
    norm_factor = 1.0 / math.sqrt(length)
    return (jnp.cos(angles) * norm_factor, -jnp.sin(angles) * norm_factor)

def kernel_table(length):
    grid_index = jnp.arange(length, dtype=jnp.int32)
    centred = (grid_index + length // 2) % length - length // 2
    squares = centred[:, None] * centred[:, None] + centred[None, :] * centred[None, :]
    phases = squares.astype(jnp.float32) * (spread_factor / length)
    return jnp.stack([jnp.cos(phases), -jnp.sin(phases)])

def left_apply(real_table, imag_table, field):

    def multiply(matrix, field_block):
        return jnp.einsum('ij,bjk->bik', matrix, field_block, precision=lax.Precision.HIGHEST)
    return jnp.stack([multiply(real_table, field[0]) - multiply(imag_table, field[1]), multiply(real_table, field[1]) + multiply(imag_table, field[0])])

def right_apply(field, real_table, imag_table):

    def multiply(field_block, matrix):
        return jnp.einsum('bij,jk->bik', field_block, matrix, precision=lax.Precision.HIGHEST)
    return jnp.stack([multiply(field[0], real_table) - multiply(field[1], imag_table), multiply(field[1], real_table) + multiply(field[0], imag_table)])

def transform(field, real_table, imag_table):
    return right_apply(left_apply(real_table, imag_table, field), real_table, imag_table)

def product(left_op, right_op):
    return jnp.stack([left_op[0] * right_op[0] - left_op[1] * right_op[1], left_op[0] * right_op[1] + left_op[1] * right_op[0]])

def conj_product(left_op, right_op):
    return jnp.stack([left_op[0] * right_op[0] + left_op[1] * right_op[1], left_op[0] * right_op[1] - left_op[1] * right_op[0]])

def propagate(field, real_table, imag_table, kernel):
    spectrum = transform(field, real_table, imag_table)
    return transform(product(kernel[:, None], spectrum), real_table, -imag_table)

def back_propagate(field, real_table, imag_table, kernel):
    spectrum = transform(field, real_table, imag_table)
    return transform(conj_product(kernel[:, None], spectrum), real_table, -imag_table)

def detector(wave_field, measured, live_mask, real_table, imag_table):
    far_field = transform(wave_field, real_table, imag_table)
    intensity = far_field[0] * far_field[0] + far_field[1] * far_field[1]
    weight = (intensity - measured) * live_mask[:, None, None]
    return transform(far_field * weight[None], real_table, -imag_table)

def rounded(field):
    return lax.optimization_barrier(field.astype(jnp.bfloat16)).astype(jnp.float32)

def reference(object_field, probe_wave, scan_coords, scan_counts, measured):
    real_table, imag_table = fourier_tables(P_SIZE)
    kernel = kernel_table(P_SIZE)
    slot_ids = jnp.arange(SLOTS, dtype=jnp.int32)
    owner_ids = slot_ids // CAP
    live_mask = (slot_ids % CAP < scan_counts[owner_ids]).astype(jnp.float32)
    zero_index = jnp.zeros((), jnp.int32)

    def one_slot(gradient, inputs):
        corner_row, corner_col, sample, weight = inputs
        corner_row = corner_row.astype(jnp.int32)
        corner_col = corner_col.astype(jnp.int32)
        offsets = (zero_index, zero_index, corner_row, corner_col)
        patches = lax.dynamic_slice(object_field, offsets, (2, SLICES, P_SIZE, P_SIZE))
        current_wave = probe_wave[:, None]
        kept_waves = []
        for layer_id in range(SLICES):
            if layer_id % SL_DEV == 0 and layer_id > 0:
                current_wave = rounded(current_wave)
            kept_waves.append(current_wave)
            current_wave = propagate(product(current_wave, patches[:, layer_id][:, None]), real_table, imag_table, kernel)
        adjoint = detector(current_wave, sample[None], weight[None], real_table, imag_table)
        pieces = [None] * SLICES
        for layer_id in reversed(range(SLICES)):
            moved = back_propagate(adjoint, real_table, imag_table, kernel)
            pieces[layer_id] = conj_product(kept_waves[layer_id], moved)[:, 0]
            adjoint = conj_product(patches[:, layer_id][:, None], moved)
            if layer_id % SL_DEV == 0 and layer_id > 0:
                adjoint = rounded(adjoint)
        stacked = jnp.stack(pieces, axis=1)
        current = lax.dynamic_slice(gradient, offsets, (2, SLICES, P_SIZE, P_SIZE))
        return (lax.dynamic_update_slice(gradient, current + stacked, offsets), None)
    gradient, unused = lax.scan(one_slot, jnp.zeros(object_field.shape, jnp.float32), (scan_coords[:, 0], scan_coords[:, 1], measured, live_mask))
    return gradient
```

```python
import jax
import jax.numpy as jnp
import numpy as np
from jax import lax
from jax.experimental import pallas as pl
from jax.experimental.pallas import tpu as pltpu
from jax.sharding import PartitionSpec as P

f32 = jnp.float32
bf16 = jnp.bfloat16
N = 128
SLICES = 8
CAP = 3
N_POS = 32
NCOL = 2048
WORKERS = (0, 2, 6)
MESH = pl.DeviceIdType.MESH


def split_bf16(values):
    high = np.asarray(values, np.float32).astype(jnp.bfloat16)
    low = (values - high.astype(np.float64)).astype(np.float32).astype(jnp.bfloat16)
    return high, low


def tables():
    j = np.arange(N)
    fourier = np.exp(-2j * np.pi * ((j[:, None] * j) % N) / N) / np.sqrt(N)
    centred = (j + N // 2) % N - N // 2
    phase = np.exp(-0.5j * centred * centred / N)
    step = fourier.conj() @ (phase[:, None] * fourier)
    out = []
    for matrix in (step, fourier):
        real_high, real_low = split_bf16(matrix.real)
        imag_high, imag_low = split_bf16(matrix.imag)
        out.append(np.block([[real_high, real_low], [imag_high, imag_low]]))
        out.append(np.block([[real_high, imag_high], [real_low, imag_low]]))
    return np.stack(out)


def sandwich(left, right, real, imag, sign):
    x = jnp.concatenate([real.astype(bf16), imag.astype(bf16)], axis=1)
    x = jnp.concatenate([x, x], axis=0)
    y = jnp.dot(left, x, preferred_element_type=f32)
    if sign > 0:
        real, imag = y[:N, :N] - y[N:, N:], y[:N, N:] + y[N:, :N]
    else:
        real, imag = y[:N, :N] + y[N:, N:], y[:N, N:] - y[N:, :N]
    x = jnp.concatenate([real.astype(bf16), imag.astype(bf16)], axis=0)
    x = jnp.concatenate([x, x], axis=1)
    y = jnp.dot(x, right, preferred_element_type=f32)
    if sign > 0:
        return y[:N, :N] - y[N:, N:], y[:N, N:] + y[N:, :N]
    return y[:N, :N] + y[N:, N:], y[N:, :N] - y[:N, N:]


def corner(coords, k, strip):
    row = coords[k, 0] - strip * N
    col = coords[k, 1]
    block = jnp.minimum(lax.shift_right_arithmetic(col, 7), NCOL // N - 2)
    return row, block, col - block * N


def gather_kernel(
    coords_ref, counts_ref, object_ref, probe_ref, measured_ref, tables_ref,
    grads_ref, info_ref,
    strip, probe, table, sample, live, live_in, coords_in,
    top_out, low_out, tops, lows, kept, grad_out,
    block_sem, load_sem, coord_sem, sample_sem, live_sem,
    top_send, top_recv, low_send, low_recv, grad_send, grad_recv, own_sem,
):
    s = lax.axis_index("slab")
    p = lax.axis_index("pos")
    after = lax.rem(p + 1, N_POS)
    before = lax.rem(p + N_POS - 1, N_POS)
    is_worker = (s == WORKERS[0]) | (s == WORKERS[1]) | (s == WORKERS[2])
    slot = s // 2 - s // 6

    def load_block(c):
        columns = pl.ds(pl.multiple_of(c * N, N), N)
        return pltpu.make_async_copy(object_ref.at[:, 0, :, columns], strip.at[c], block_sem.at[c])

    def start_block(c, carry):
        load_block(c).start()
        return carry

    def wait_block(c, carry):
        load_block(c).wait()
        return carry

    lax.fori_loop(0, NCOL // N, start_block, 0)
    load_probe = pltpu.make_async_copy(probe_ref, probe, load_sem.at[1])
    load_table = pltpu.make_async_copy(tables_ref, table, load_sem.at[2])

    barrier = pltpu.get_barrier_semaphore()

    def greet(where):
        pl.semaphore_signal(barrier, inc=1, device_id=where, device_id_type=MESH)

    greet((s, after))
    greet((s, before))
    for w in WORKERS:
        greet((w, after))

        @pl.when(s != w)
        def _():
            greet((w, p))

    @pl.when(is_worker)
    def _():
        load_probe.start()
        load_table.start()
        for other in range(SLICES):
            greet((other, before))

            @pl.when(s != other)
            def _():
                greet((other, p))

    @pl.when(is_worker)
    def _():
        pl.semaphore_wait(barrier, 22)

    @pl.when(jnp.logical_not(is_worker))
    def _():
        pl.semaphore_wait(barrier, 8)

    def send(src, dst, send_sem, recv_sem, where):
        return pltpu.make_async_remote_copy(
            src_ref=src, dst_ref=dst, send_sem=send_sem, recv_sem=recv_sem,
            device_id=where, device_id_type=MESH,
        )

    coord_copy = send(coords_ref, coords_in, coord_sem.at[0], coord_sem.at[1], (s, after))
    coord_copy.start()

    def sample_copy(k):
        return send(measured_ref.at[k], sample, sample_sem.at[0], sample_sem.at[1], (s, after))

    live_copy = send(live, live_in, live_sem.at[0], live_sem.at[1], (s, after))
    for k, w in enumerate(WORKERS):

        @pl.when(s == w)
        def _():
            sample_copy(k).start()
            live[...] = jnp.clip(jnp.full((8, N), counts_ref[0] - k, jnp.int32), 0, 1).astype(f32)
            live_copy.start()

    row_id = lax.broadcasted_iota(jnp.int32, (N, N), 0)
    lane_id = lax.broadcasted_iota(jnp.int32, (N, N), 1)
    window_row = lax.broadcasted_iota(jnp.int32, (2 * N, N), 0)
    window_lane = lax.broadcasted_iota(jnp.int32, (2 * N, N), 1)

    def one_hot(where):
        return jnp.where(where, 1.0, 0.0).astype(bf16)

    def cut(first_row, block, shift, dst, k):
        near = strip[block]
        far = strip[block + 1]
        real = jnp.concatenate([near[0] - 1.0, far[0] - 1.0], axis=1)
        imag = jnp.concatenate([near[1], far[1]], axis=1)
        window = jnp.concatenate([real.astype(bf16), imag.astype(bf16)], axis=0)
        moved = one_hot(window_row == window_lane + shift)
        tile = jnp.dot(window, moved, preferred_element_type=f32).astype(bf16)
        tile = jnp.concatenate([tile[:N], tile[N:]], axis=1)
        moved = one_hot(lane_id == row_id + first_row)
        tile = jnp.dot(moved, tile, preferred_element_type=f32).astype(bf16)
        dst[k, 0] = tile[:, :N]
        dst[k, 1] = tile[:, N:]

    lax.fori_loop(0, NCOL // N, wait_block, 0)
    own = coords_ref[...]
    for k, w in enumerate(WORKERS):
        row, block, shift = corner(own, k, p)
        cut(row, block, shift, top_out, k)
        send(top_out.at[k], tops.at[s], top_send.at[k], top_recv.at[s], (w, after)).start()

    coord_copy.wait_recv()
    theirs = coords_in[...]
    info_ref[0] = own
    info_ref[1] = theirs
    for k, w in enumerate(WORKERS):
        row, block, shift = corner(theirs, k, before)
        cut(row - N, block, shift, low_out, k)

        @pl.when(s != w)
        def _():
            send(low_out.at[k], lows.at[s], low_send.at[k], low_recv.at[s], (w, p)).start()

        @pl.when(s == w)
        def _():
            lows[s] = low_out[k]

    @pl.when(is_worker)
    def _():
        load_probe.wait()
        load_table.wait()

        def patch(i):
            return (
                tops[i, 0].astype(f32) + lows[i, 0].astype(f32),
                tops[i, 1].astype(f32) + lows[i, 1].astype(f32),
            )

        def arrive(i):
            send(top_out.at[0], tops.at[i], top_send.at[0], top_recv.at[i], (s, after)).wait_recv()

            @pl.when(i != s)
            def _():
                send(low_out.at[0], lows.at[i], low_send.at[0], low_recv.at[i], (s, p)).wait_recv()

        def through(i, real, imag):
            kept[i, 0] = real
            kept[i, 1] = imag
            arrive(i)
            d_real, d_imag = patch(i)
            return (
                real + (real * d_real - imag * d_imag),
                imag + (real * d_imag + imag * d_real),
            )

        def forward(i, wave):
            return sandwich(table[0], table[1], *through(i, *wave), 1)

        wave = lax.fori_loop(0, SLICES - 1, forward, (probe[0], probe[1]))
        real, imag = sandwich(table[2], table[3], *through(SLICES - 1, *wave), 1)
        sample_copy(0).wait_recv()
        live_copy.wait_recv()
        weight = (real * real + imag * imag - sample[...]) * live_in[0:1, :]
        moved = sandwich(table[2], table[3], weight * real, weight * imag, -1)

        def emit(i, moved):
            real, imag = moved
            grad_out[i, 0] = (kept[i, 0] * real + kept[i, 1] * imag).astype(bf16)
            grad_out[i, 1] = (kept[i, 0] * imag - kept[i, 1] * real).astype(bf16)
            send(
                grad_out.at[i], grads_ref.at[slot], grad_send.at[i, 0], grad_recv.at[slot], (i, before)
            ).start()

            @pl.when(i != s)
            def _():
                send(
                    grad_out.at[i], grads_ref.at[CAP + slot], grad_send.at[i, 1],
                    grad_recv.at[CAP + slot], (i, p),
                ).start()

            @pl.when(i == s)
            def _():
                pltpu.make_async_copy(grad_out.at[i], grads_ref.at[CAP + slot], own_sem).start()

        def backward(step, moved):
            i = SLICES - 1 - step
            emit(i, moved)
            real, imag = moved
            d_real, d_imag = patch(i)
            return sandwich(
                table[0], table[1],
                real + (d_real * real + d_imag * imag),
                imag + (d_real * imag - d_imag * real),
                -1,
            )

        emit(0, lax.fori_loop(0, SLICES - 1, backward, moved))

    for k, w in enumerate(WORKERS):
        here = grad_out.at[0]
        send(here, grads_ref.at[k], grad_send.at[0, 0], grad_recv.at[k], (s, after)).wait_recv()

        @pl.when(s != w)
        def _():
            send(
                here, grads_ref.at[CAP + k], grad_send.at[0, 0], grad_recv.at[CAP + k], (s, after)
            ).wait_recv()
            send(low_out.at[k], lows.at[s], low_send.at[k], low_recv.at[s], (w, p)).wait_send()

        @pl.when(s == w)
        def _():
            pltpu.make_async_copy(here, grads_ref.at[CAP + k], own_sem).wait()
            sample_copy(k).wait_send()
            live_copy.wait_send()

        send(top_out.at[k], tops.at[s], top_send.at[k], top_recv.at[s], (w, after)).wait_send()

    coord_copy.wait_send()

    @pl.when(is_worker)
    def _():
        def drain(i, carry):
            send(grad_out.at[i], grads_ref.at[slot], grad_send.at[i, 0], grad_recv.at[slot], (i, before)).wait_send()

            @pl.when(i != s)
            def _():
                send(
                    grad_out.at[i], grads_ref.at[CAP + slot], grad_send.at[i, 1],
                    grad_recv.at[CAP + slot], (i, p),
                ).wait_send()

            return carry

        lax.fori_loop(0, SLICES, drain, 0)


def scatter_kernel(info_ref, grads_ref, out_ref, total, sem):
    p = lax.axis_index("pos")
    before = lax.rem(p + N_POS - 1, N_POS)
    total[...] = jnp.zeros((2, N, NCOL), f32)
    row_id = lax.broadcasted_iota(jnp.int32, (N, N), 0)
    lane_id = lax.broadcasted_iota(jnp.int32, (N, N), 1)
    for side in range(2):
        coords = info_ref[side]
        for k in range(CAP):
            row, block, shift = corner(coords, k, p if side == 0 else before)
            keep = row_id >= row if side == 0 else row_id < row
            base = pl.multiple_of(block * N, N)
            near = pl.ds(base, N)
            far = pl.ds(pl.multiple_of(base + N, N), N)
            turn = lax.rem(shift, N)
            for part in range(2):
                tile = pltpu.roll(grads_ref[side * CAP + k, part].astype(f32), turn, 1)
                tile = jnp.where(keep, pltpu.roll(tile, row, 0), 0.0)
                total[part, :, near] += jnp.where(lane_id >= shift, tile, 0.0)
                total[part, :, far] += jnp.where(lane_id < shift, tile, 0.0)
    store = pltpu.make_async_copy(total, out_ref.at[:, 0], sem)
    store.start()
    store.wait()


def per_device(object_field, probe_wave, scan_coords, scan_counts, measured):
    vmem = pl.BlockSpec(memory_space=pltpu.VMEM)
    smem = pl.BlockSpec(memory_space=pltpu.SMEM)
    anywhere = pl.BlockSpec(memory_space=pl.ANY)
    hbm = pl.BlockSpec(memory_space=pltpu.HBM)
    dma = pltpu.SemaphoreType.DMA
    grads, info = pl.pallas_call(
        gather_kernel,
        out_shape=(
            jax.ShapeDtypeStruct((2 * CAP, 2, N, N), bf16),
            jax.ShapeDtypeStruct((2, CAP, 2), jnp.int32),
        ),
        in_specs=[vmem, smem, hbm, hbm, hbm, hbm],
        out_specs=(anywhere, vmem),
        scratch_shapes=[
            pltpu.VMEM((NCOL // N, 2, N, N), f32),
            pltpu.VMEM((2, N, N), f32),
            pltpu.VMEM((4, 2 * N, 2 * N), bf16),
            pltpu.VMEM((N, N), f32),
            pltpu.VMEM((8, N), f32),
            pltpu.VMEM((8, N), f32),
            pltpu.VMEM((CAP, 2), jnp.int32),
            pltpu.VMEM((CAP, 2, N, N), bf16),
            pltpu.VMEM((CAP, 2, N, N), bf16),
            pltpu.VMEM((SLICES, 2, N, N), bf16),
            pltpu.VMEM((SLICES, 2, N, N), bf16),
            pltpu.VMEM((SLICES, 2, N, N), f32),
            pltpu.VMEM((SLICES, 2, N, N), bf16),
            dma((NCOL // N,)), dma((3,)), dma((2,)), dma((2,)), dma((2,)),
            dma((CAP,)), dma((SLICES,)), dma((CAP,)), dma((SLICES,)),
            dma((SLICES, 2)), dma((2 * CAP,)), dma,
        ],
        compiler_params=pltpu.CompilerParams(
            collective_id=0, has_side_effects=True, vmem_limit_bytes=60 << 20
        ),
        name="chain",
    )(scan_coords, scan_counts, object_field, probe_wave, measured, jnp.asarray(tables()))
    return pl.pallas_call(
        scatter_kernel,
        out_shape=jax.ShapeDtypeStruct(object_field.shape, f32),
        in_specs=[vmem, vmem],
        out_specs=anywhere,
        scratch_shapes=[pltpu.VMEM((2, N, NCOL), f32), dma],
        compiler_params=pltpu.CompilerParams(vmem_limit_bytes=40 << 20),
        name="scatter",
    )(info, grads)


def solution(mesh):
    in_specs = (P(None, "slab", "pos", None), P(), P("pos", None), P("pos"), P("pos", None, None))
    out_specs = P(None, "slab", "pos", None)
    return jax.shard_map(
        per_device, mesh=mesh, in_specs=in_specs, out_specs=out_specs, check_vma=False
    )
```

```python
import jax
import jax.numpy as jnp
import numpy as np
from jax import lax
from jax.experimental import pallas as pl
from jax.experimental.pallas import tpu as pltpu
from jax.sharding import PartitionSpec as P

f32 = jnp.float32
bf16 = jnp.bfloat16
N = 128
SLICES = 8
CAP = 3
NCOL = 2048
WORKERS = (0, 2, 6)
MESH = pl.DeviceIdType.MESH


def split_bf16(values):
    high = np.asarray(values, np.float32).astype(jnp.bfloat16)
    low = (values - high.astype(np.float64)).astype(np.float32).astype(jnp.bfloat16)
    return high, low


def tables():
    j = np.arange(N)
    fourier = np.exp(-2j * np.pi * ((j[:, None] * j) % N) / N) / np.sqrt(N)
    centred = (j + N // 2) % N - N // 2
    phase = np.exp(-0.5j * centred * centred / N)
    step = fourier.conj() @ (phase[:, None] * fourier)
    out = []
    for matrix in (step, fourier):
        real_high, real_low = split_bf16(matrix.real)
        imag_high, imag_low = split_bf16(matrix.imag)
        out.append(np.block([[real_high, real_low], [imag_high, imag_low]]))
        out.append(np.block([[real_high, imag_high], [real_low, imag_low]]))
    return np.stack(out)


def sandwich(left, right, real, imag, sign):
    x = jnp.concatenate([real.astype(bf16), imag.astype(bf16)], axis=1)
    x = jnp.concatenate([x, x], axis=0)
    y = jnp.dot(left, x, preferred_element_type=f32)
    if sign > 0:
        real, imag = y[:N, :N] - y[N:, N:], y[:N, N:] + y[N:, :N]
    else:
        real, imag = y[:N, :N] + y[N:, N:], y[:N, N:] - y[N:, :N]
    x = jnp.concatenate([real.astype(bf16), imag.astype(bf16)], axis=0)
    x = jnp.concatenate([x, x], axis=1)
    y = jnp.dot(x, right, preferred_element_type=f32)
    if sign > 0:
        return y[:N, :N] - y[N:, N:], y[:N, N:] + y[N:, :N]
    return y[:N, :N] + y[N:, N:], y[N:, :N] - y[:N, N:]


def corner(coords, k, strip):
    row = coords[0, k] - strip * N
    col = coords[1, k]
    block = jnp.minimum(lax.shift_right_arithmetic(col, 7), NCOL // N - 2)
    return row, block, col - block * N


def gather_kernel(
    coords_ref, counts_ref, object_ref, probe_ref, measured_ref, tables_ref,
    grads_ref, info_ref,
    strip, probe, table, sample, live, live_in, coords_in,
    top_out, low_out, tops, lows, kept, grad_out,
    block_sem, load_sem, coord_sem, sample_sem, live_sem,
    top_send, top_recv, low_send, low_recv, grad_send, grad_recv, own_sem,
):
    s = lax.axis_index("slab")
    p = lax.axis_index("pos")
    strips = lax.axis_size("pos")
    after = lax.rem(p + 1, strips)
    before = lax.rem(p + strips - 1, strips)
    is_worker = (s == WORKERS[0]) | (s == WORKERS[1]) | (s == WORKERS[2])
    slot = s // 2 - s // 6

    def load_block(c):
        columns = pl.ds(pl.multiple_of(c * N, N), N)
        return pltpu.make_async_copy(object_ref.at[:, 0, :, columns], strip.at[c], block_sem.at[c])

    def start_block(c, carry):
        load_block(c).start()
        return carry

    def wait_block(c, carry):
        load_block(c).wait()
        return carry

    lax.fori_loop(0, NCOL // N, start_block, 0)
    load_probe = pltpu.make_async_copy(probe_ref, probe, load_sem.at[1])
    load_table = pltpu.make_async_copy(tables_ref, table, load_sem.at[2])

    barrier = pltpu.get_barrier_semaphore()

    def greet(where):
        pl.semaphore_signal(barrier, inc=1, device_id=where, device_id_type=MESH)

    greet((s, after))
    greet((s, before))
    for w in WORKERS:
        greet((w, after))

        @pl.when(s != w)
        def _():
            greet((w, p))

    @pl.when(is_worker)
    def _():
        load_probe.start()
        load_table.start()
        for other in range(SLICES):
            greet((other, before))

            @pl.when(s != other)
            def _():
                greet((other, p))

    @pl.when(is_worker)
    def _():
        pl.semaphore_wait(barrier, 22)

    @pl.when(jnp.logical_not(is_worker))
    def _():
        pl.semaphore_wait(barrier, 8)

    def send(src, dst, send_sem, recv_sem, where):
        return pltpu.make_async_remote_copy(
            src_ref=src, dst_ref=dst, send_sem=send_sem, recv_sem=recv_sem,
            device_id=where, device_id_type=MESH,
        )

    coord_copy = send(coords_ref, coords_in, coord_sem.at[0], coord_sem.at[1], (s, after))
    coord_copy.start()

    def sample_copy(k):
        return send(measured_ref.at[k], sample, sample_sem.at[0], sample_sem.at[1], (s, after))

    live_copy = send(live, live_in, live_sem.at[0], live_sem.at[1], (s, after))
    for k, w in enumerate(WORKERS):

        @pl.when(s == w)
        def _():
            sample_copy(k).start()
            live[...] = jnp.clip(jnp.full((8, N), counts_ref[0] - k, jnp.int32), 0, 1).astype(f32)
            live_copy.start()

    row_id = lax.broadcasted_iota(jnp.int32, (N, N), 0)
    lane_id = lax.broadcasted_iota(jnp.int32, (N, N), 1)

    def cut(keep, block, shift, dst, k):
        near = strip[block]
        far = strip[block + 1]
        for part in range(2):
            tile = jnp.where(lane_id >= shift, near[part], far[part])
            if part == 0:
                tile = tile - 1.0
            dst[k, part] = jnp.where(keep, tile, 0.0).astype(bf16)

    lax.fori_loop(0, NCOL // N, wait_block, 0)
    own = coords_ref[...]
    for k, w in enumerate(WORKERS):
        row, block, shift = corner(own, k, p)
        cut(row_id >= row, block, shift, top_out, k)
        send(top_out.at[k], tops.at[s], top_send.at[k], top_recv.at[s], (w, after)).start()

    coord_copy.wait_recv()
    theirs = coords_in[...]
    info_ref[...] = theirs
    corners = [corner(theirs, k, before) for k in range(CAP)]
    for k, w in enumerate(WORKERS):
        row, block, shift = corners[k]
        cut(row_id < row, block, shift, low_out, k)

        @pl.when(s != w)
        def _():
            send(low_out.at[k], lows.at[s], low_send.at[k], low_recv.at[s], (w, p)).start()

        @pl.when(s == w)
        def _():
            lows[s] = low_out[k]

    @pl.when(is_worker)
    def _():
        load_probe.wait()
        load_table.wait()

        def patch(i):
            return (
                tops[i, 0].astype(f32) + lows[i, 0].astype(f32),
                tops[i, 1].astype(f32) + lows[i, 1].astype(f32),
            )

        def arrive(i):
            send(top_out.at[0], tops.at[i], top_send.at[0], top_recv.at[i], (s, after)).wait_recv()

            @pl.when(i != s)
            def _():
                send(low_out.at[0], lows.at[i], low_send.at[0], low_recv.at[i], (s, p)).wait_recv()

        def through(i, real, imag):
            kept[i, 0] = real
            kept[i, 1] = imag
            arrive(i)
            d_real, d_imag = patch(i)
            return (
                real + (real * d_real - imag * d_imag),
                imag + (real * d_imag + imag * d_real),
            )

        def forward(i, wave):
            return sandwich(table[0], table[1], *through(i, *wave), 1)

        row = jnp.where(slot == 0, corners[0][0], jnp.where(slot == 1, corners[1][0], corners[2][0]))
        shift = jnp.where(slot == 0, corners[0][2], jnp.where(slot == 1, corners[1][2], corners[2][2]))

        def turned(x):
            return pltpu.roll(pltpu.roll(x, lax.rem(shift, N), 1), row, 0)

        wave = lax.fori_loop(0, SLICES - 1, forward, (turned(probe[0]), turned(probe[1])))
        real, imag = sandwich(table[2], table[3], *through(SLICES - 1, *wave), 1)
        sample_copy(0).wait_recv()
        live_copy.wait_recv()
        weight = (real * real + imag * imag - sample[...]) * live_in[0:1, :]
        moved = sandwich(table[2], table[3], weight * real, weight * imag, -1)

        def emit(i, moved):
            real, imag = moved
            grad_out[i, 0] = (kept[i, 0] * real + kept[i, 1] * imag).astype(bf16)
            grad_out[i, 1] = (kept[i, 0] * imag - kept[i, 1] * real).astype(bf16)
            send(
                grad_out.at[i], grads_ref.at[slot], grad_send.at[i, 0], grad_recv.at[slot], (i, before)
            ).start()

            @pl.when(i != s)
            def _():
                send(
                    grad_out.at[i], grads_ref.at[CAP + slot], grad_send.at[i, 1],
                    grad_recv.at[CAP + slot], (i, p),
                ).start()

            @pl.when(i == s)
            def _():
                pltpu.make_async_copy(grad_out.at[i], grads_ref.at[CAP + slot], own_sem).start()

        def backward(step, moved):
            i = SLICES - 1 - step
            emit(i, moved)
            real, imag = moved
            d_real, d_imag = patch(i)
            return sandwich(
                table[0], table[1],
                real + (d_real * real + d_imag * imag),
                imag + (d_real * imag - d_imag * real),
                -1,
            )

        emit(0, lax.fori_loop(0, SLICES - 1, backward, moved))

    for k, w in enumerate(WORKERS):
        here = grad_out.at[0]
        send(here, grads_ref.at[k], grad_send.at[0, 0], grad_recv.at[k], (s, after)).wait_recv()

        @pl.when(s != w)
        def _():
            send(
                here, grads_ref.at[CAP + k], grad_send.at[0, 0], grad_recv.at[CAP + k], (s, after)
            ).wait_recv()
            send(low_out.at[k], lows.at[s], low_send.at[k], low_recv.at[s], (w, p)).wait_send()

        @pl.when(s == w)
        def _():
            pltpu.make_async_copy(here, grads_ref.at[CAP + k], own_sem).wait()
            sample_copy(k).wait_send()
            live_copy.wait_send()

        send(top_out.at[k], tops.at[s], top_send.at[k], top_recv.at[s], (w, after)).wait_send()

    coord_copy.wait_send()

    @pl.when(is_worker)
    def _():
        def drain(i, carry):
            send(grad_out.at[i], grads_ref.at[slot], grad_send.at[i, 0], grad_recv.at[slot], (i, before)).wait_send()

            @pl.when(i != s)
            def _():
                send(
                    grad_out.at[i], grads_ref.at[CAP + slot], grad_send.at[i, 1],
                    grad_recv.at[CAP + slot], (i, p),
                ).wait_send()

            return carry

        lax.fori_loop(0, SLICES, drain, 0)


def scatter_kernel(own_ref, their_ref, grads_ref, out_ref, total, sem):
    p = lax.axis_index("pos")
    before = lax.rem(p + lax.axis_size("pos") - 1, lax.axis_size("pos"))
    total[...] = jnp.zeros((2, N, NCOL), f32)
    row_id = lax.broadcasted_iota(jnp.int32, (N, N), 0)
    lane_id = lax.broadcasted_iota(jnp.int32, (N, N), 1)
    for side in range(2):
        coords = own_ref[...] if side == 0 else their_ref[...]
        for k in range(CAP):
            row, block, shift = corner(coords, k, p if side == 0 else before)
            keep = row_id >= row if side == 0 else row_id < row
            base = pl.multiple_of(block * N, N)
            near = pl.ds(base, N)
            far = pl.ds(pl.multiple_of(base + N, N), N)
            for part in range(2):
                tile = jnp.where(keep, grads_ref[side * CAP + k, part].astype(f32), 0.0)
                total[part, :, near] += jnp.where(lane_id >= shift, tile, 0.0)
                total[part, :, far] += jnp.where(lane_id < shift, tile, 0.0)
    store = pltpu.make_async_copy(total, out_ref.at[:, 0], sem)
    store.start()
    store.wait()


def per_device(object_field, probe_wave, scan_coords, scan_counts, measured):
    vmem = pl.BlockSpec(memory_space=pltpu.VMEM)
    smem = pl.BlockSpec(memory_space=pltpu.SMEM)
    anywhere = pl.BlockSpec(memory_space=pl.ANY)
    hbm = pl.BlockSpec(memory_space=pltpu.HBM)
    dma = pltpu.SemaphoreType.DMA
    coords = scan_coords.T
    grads, theirs = pl.pallas_call(
        gather_kernel,
        out_shape=(
            pltpu.VMEM((2 * CAP, 2, N, N), bf16),
            pltpu.VMEM((2, CAP), jnp.int32),
        ),
        in_specs=[vmem, smem, hbm, hbm, hbm, hbm],
        out_specs=(vmem, vmem),
        scratch_shapes=[
            pltpu.VMEM((NCOL // N, 2, N, N), f32),
            pltpu.VMEM((2, N, N), f32),
            pltpu.VMEM((4, 2 * N, 2 * N), bf16),
            pltpu.VMEM((N, N), f32),
            pltpu.VMEM((8, N), f32),
            pltpu.VMEM((8, N), f32),
            pltpu.VMEM((2, CAP), jnp.int32),
            pltpu.VMEM((CAP, 2, N, N), bf16),
            pltpu.VMEM((CAP, 2, N, N), bf16),
            pltpu.VMEM((SLICES, 2, N, N), bf16),
            pltpu.VMEM((SLICES, 2, N, N), bf16),
            pltpu.VMEM((SLICES, 2, N, N), f32),
            pltpu.VMEM((SLICES, 2, N, N), bf16),
            dma((NCOL // N,)), dma((3,)), dma((2,)), dma((2,)), dma((2,)),
            dma((CAP,)), dma((SLICES,)), dma((CAP,)), dma((SLICES,)),
            dma((SLICES, 2)), dma((2 * CAP,)), dma,
        ],
        compiler_params=pltpu.CompilerParams(
            collective_id=0, has_side_effects=True, vmem_limit_bytes=60 << 20
        ),
        name="chain",
    )(coords, scan_counts, object_field, probe_wave, measured, jnp.asarray(tables()))
    return pl.pallas_call(
        scatter_kernel,
        out_shape=jax.ShapeDtypeStruct(object_field.shape, f32),
        in_specs=[vmem, vmem, vmem],
        out_specs=anywhere,
        scratch_shapes=[pltpu.VMEM((2, N, NCOL), f32), dma],
        compiler_params=pltpu.CompilerParams(vmem_limit_bytes=40 << 20),
        name="scatter",
    )(coords, theirs, grads)


def solution(mesh):
    in_specs = (P(None, "slab", "pos", None), P(), P("pos", None), P("pos"), P("pos", None, None))
    out_specs = P(None, "slab", "pos", None)
    return jax.shard_map(
        per_device, mesh=mesh, in_specs=in_specs, out_specs=out_specs, check_vma=False
    )
```

```python
import jax
import jax.numpy as jnp
import numpy as np
from jax import lax
from jax.experimental import pallas as pl
from jax.experimental.pallas import tpu as pltpu
from jax.sharding import PartitionSpec as P

f32 = jnp.float32
bf16 = jnp.bfloat16
N = 128
SLICES = 8
CAP = 3
NCOL = 2048
WORKERS = (0, 2, 4)
ORDER = (2, 1, 0)
MESH = pl.DeviceIdType.MESH


def split_bf16(values):
    high = np.asarray(values, np.float32).astype(jnp.bfloat16)
    low = (values - high.astype(np.float64)).astype(np.float32).astype(jnp.bfloat16)
    return high, low


def tables():
    j = np.arange(N)
    fourier = np.exp(-2j * np.pi * ((j[:, None] * j) % N) / N) / np.sqrt(N)
    centred = (j + N // 2) % N - N // 2
    phase = np.exp(-0.5j * centred * centred / N)
    step = fourier.conj() @ (phase[:, None] * fourier)
    out = []
    for matrix in (step, fourier):
        real_high, real_low = split_bf16(matrix.real)
        imag_high, imag_low = split_bf16(matrix.imag)
        out.append(np.block([[real_high, real_low], [imag_high, imag_low]]))
        out.append(np.block([[real_high, imag_high], [real_low, imag_low]]))
    return np.stack(out)


def sandwich(left, right, real, imag, sign):
    x = jnp.concatenate([real.astype(bf16), imag.astype(bf16)], axis=1)
    x = jnp.concatenate([x, x], axis=0)
    y = jnp.dot(left, x, preferred_element_type=f32)
    if sign > 0:
        real, imag = y[:N, :N] - y[N:, N:], y[:N, N:] + y[N:, :N]
    else:
        real, imag = y[:N, :N] + y[N:, N:], y[:N, N:] - y[N:, :N]
    x = jnp.concatenate([real.astype(bf16), imag.astype(bf16)], axis=0)
    x = jnp.concatenate([x, x], axis=1)
    y = jnp.dot(x, right, preferred_element_type=f32)
    if sign > 0:
        return y[:N, :N] - y[N:, N:], y[:N, N:] + y[N:, :N]
    return y[:N, :N] + y[N:, N:], y[N:, :N] - y[:N, N:]


def corner(coords, k, strip):
    row = coords[0, k] - strip * N
    col = coords[1, k]
    block = jnp.minimum(lax.shift_right_arithmetic(col, 7), NCOL // N - 2)
    return row, block, col - block * N


def gather_kernel(
    coords_hbm, counts_hbm, object_ref, probe_ref, measured_ref, tables_ref,
    grads_ref, info_ref,
    coords_ref, counts_ref, strip, probe, table, sample, live, live_in, coords_in,
    top_out, low_out, tops, lows, kept, grad_out,
    block_sem, load_sem, coord_sem, sample_sem, live_sem,
    top_send, top_recv, low_send, low_recv, grad_send, grad_recv, own_sem,
):
    s = lax.axis_index("slab")
    p = lax.axis_index("pos")
    strips = lax.axis_size("pos")
    after = lax.rem(p + 1, strips)
    before = lax.rem(p + strips - 1, strips)
    is_worker = (s == WORKERS[0]) | (s == WORKERS[1]) | (s == WORKERS[2])
    slot = s // 2

    load_coords = pltpu.make_async_copy(coords_hbm, coords_ref, load_sem.at[2])
    load_counts = pltpu.make_async_copy(counts_hbm, counts_ref, load_sem.at[3])
    load_coords.start()
    barrier = pltpu.get_barrier_semaphore()

    def greet(where):
        pl.semaphore_signal(barrier, inc=1, device_id=where, device_id_type=MESH)

    for w in WORKERS:
        greet((w, after))

        @pl.when(s != w)
        def _():
            greet((w, p))

    @pl.when(is_worker)
    def _():
        for other in range(SLICES):
            greet((other, before))

            @pl.when(s != other)
            def _():
                greet((other, p))

    greet((s, after))
    greet((s, before))

    def load_block(c):
        columns = pl.ds(pl.multiple_of(c * N, N), N)
        return pltpu.make_async_copy(object_ref.at[:, 0, :, columns], strip.at[c], block_sem.at[c])

    def start_block(c, carry):
        load_block(c).start()
        return carry

    def wait_block(c, carry):
        load_block(c).wait()
        return carry

    lax.fori_loop(0, NCOL // N, start_block, 0)
    load_probe = pltpu.make_async_copy(probe_ref, probe, load_sem.at[0])
    load_table = pltpu.make_async_copy(tables_ref, table, load_sem.at[1])

    @pl.when(is_worker)
    def _():
        load_probe.start()
        load_table.start()
        load_counts.start()
        pl.semaphore_wait(barrier, 22)

    @pl.when(jnp.logical_not(is_worker))
    def _():
        pl.semaphore_wait(barrier, 8)

    def send(src, dst, send_sem, recv_sem, where):
        return pltpu.make_async_remote_copy(
            src_ref=src, dst_ref=dst, send_sem=send_sem, recv_sem=recv_sem,
            device_id=where, device_id_type=MESH,
        )

    coord_copy = send(coords_ref, coords_in, coord_sem.at[0], coord_sem.at[1], (s, after))
    load_coords.wait()
    coord_copy.start()

    def sample_copy(k):
        return send(measured_ref.at[k], sample, sample_sem.at[0], sample_sem.at[1], (s, after))

    live_copy = send(live, live_in, live_sem.at[0], live_sem.at[1], (s, after))
    row_id = lax.broadcasted_iota(jnp.int32, (N, N), 0)
    lane_id = lax.broadcasted_iota(jnp.int32, (N, N), 1)

    def cut(keep, block, shift, dst, k):
        near = strip[block]
        far = strip[block + 1]
        for part in range(2):
            tile = jnp.where(lane_id >= shift, near[part], far[part])
            if part == 0:
                tile = tile - 1.0
            dst[k, part] = jnp.where(keep, tile, 0.0).astype(bf16)

    lax.fori_loop(0, NCOL // N, wait_block, 0)
    own = coords_ref[...]
    for k in ORDER:
        w = WORKERS[k]
        row, block, shift = corner(own, k, p)
        cut(row_id >= row, block, shift, top_out, k)
        send(top_out.at[k], tops.at[s], top_send.at[k], top_recv.at[s], (w, after)).start()

    coord_copy.wait_recv()
    theirs = coords_in[...]
    info_ref[...] = theirs
    corners = [corner(theirs, k, before) for k in range(CAP)]
    for k in ORDER:
        w = WORKERS[k]
        row, block, shift = corners[k]
        cut(row_id < row, block, shift, low_out, k)

        @pl.when(s != w)
        def _():
            send(low_out.at[k], lows.at[s], low_send.at[k], low_recv.at[s], (w, p)).start()

        @pl.when(s == w)
        def _():
            lows[s] = low_out[k]

    @pl.when(is_worker)
    def _():
        load_counts.wait()

    for k, w in enumerate(WORKERS):

        @pl.when(s == w)
        def _():
            sample_copy(k).start()
            live[...] = jnp.clip(jnp.full((8, N), counts_ref[0] - k, jnp.int32), 0, 1).astype(f32)
            live_copy.start()

    @pl.when(is_worker)
    def _():
        load_probe.wait()
        load_table.wait()

        def patch(i):
            return (
                tops[i, 0].astype(f32) + lows[i, 0].astype(f32),
                tops[i, 1].astype(f32) + lows[i, 1].astype(f32),
            )

        def arrive(i):
            send(top_out.at[0], tops.at[i], top_send.at[0], top_recv.at[i], (s, after)).wait_recv()

            @pl.when(i != s)
            def _():
                send(low_out.at[0], lows.at[i], low_send.at[0], low_recv.at[i], (s, p)).wait_recv()

        def through(i, real, imag):
            kept[i, 0] = real
            kept[i, 1] = imag
            arrive(i)
            d_real, d_imag = patch(i)
            return (
                real + (real * d_real - imag * d_imag),
                imag + (real * d_imag + imag * d_real),
            )

        def forward(i, wave):
            return sandwich(table[0], table[1], *through(i, *wave), 1)

        row = jnp.where(slot == 0, corners[0][0], jnp.where(slot == 1, corners[1][0], corners[2][0]))
        shift = jnp.where(slot == 0, corners[0][2], jnp.where(slot == 1, corners[1][2], corners[2][2]))

        def turned(x):
            return pltpu.roll(pltpu.roll(x, lax.rem(shift, N), 1), row, 0)

        wave = lax.fori_loop(0, SLICES - 1, forward, (turned(probe[0]), turned(probe[1])))
        real, imag = sandwich(table[2], table[3], *through(SLICES - 1, *wave), 1)
        sample_copy(0).wait_recv()
        live_copy.wait_recv()
        weight = (real * real + imag * imag - sample[...]) * live_in[0:1, :]
        moved = sandwich(table[2], table[3], weight * real, weight * imag, -1)

        def emit(i, moved):
            real, imag = moved
            grad_out[i, 0] = (kept[i, 0] * real + kept[i, 1] * imag).astype(bf16)
            grad_out[i, 1] = (kept[i, 0] * imag - kept[i, 1] * real).astype(bf16)
            send(
                grad_out.at[i], grads_ref.at[slot], grad_send.at[i, 0], grad_recv.at[slot], (i, before)
            ).start()

            @pl.when(i != s)
            def _():
                send(
                    grad_out.at[i], grads_ref.at[CAP + slot], grad_send.at[i, 1],
                    grad_recv.at[CAP + slot], (i, p),
                ).start()

            @pl.when(i == s)
            def _():
                pltpu.make_async_copy(grad_out.at[i], grads_ref.at[CAP + slot], own_sem).start()

        def backward(step, moved):
            i = SLICES - 1 - step
            emit(i, moved)
            real, imag = moved
            d_real, d_imag = patch(i)
            return sandwich(
                table[0], table[1],
                real + (d_real * real + d_imag * imag),
                imag + (d_real * imag - d_imag * real),
                -1,
            )

        emit(0, lax.fori_loop(0, SLICES - 1, backward, moved))

    for k, w in enumerate(WORKERS):
        here = grad_out.at[0]
        send(here, grads_ref.at[k], grad_send.at[0, 0], grad_recv.at[k], (s, after)).wait_recv()

        @pl.when(s != w)
        def _():
            send(
                here, grads_ref.at[CAP + k], grad_send.at[0, 0], grad_recv.at[CAP + k], (s, after)
            ).wait_recv()
            send(low_out.at[k], lows.at[s], low_send.at[k], low_recv.at[s], (w, p)).wait_send()

        @pl.when(s == w)
        def _():
            pltpu.make_async_copy(here, grads_ref.at[CAP + k], own_sem).wait()
            sample_copy(k).wait_send()
            live_copy.wait_send()

        send(top_out.at[k], tops.at[s], top_send.at[k], top_recv.at[s], (w, after)).wait_send()

    coord_copy.wait_send()

    @pl.when(is_worker)
    def _():
        def drain(i, carry):
            send(grad_out.at[i], grads_ref.at[slot], grad_send.at[i, 0], grad_recv.at[slot], (i, before)).wait_send()

            @pl.when(i != s)
            def _():
                send(
                    grad_out.at[i], grads_ref.at[CAP + slot], grad_send.at[i, 1],
                    grad_recv.at[CAP + slot], (i, p),
                ).wait_send()

            return carry

        lax.fori_loop(0, SLICES, drain, 0)


def scatter_kernel(own_ref, their_ref, grads_ref, out_ref, total, sem):
    p = lax.axis_index("pos")
    before = lax.rem(p + lax.axis_size("pos") - 1, lax.axis_size("pos"))
    row_id = lax.broadcasted_iota(jnp.int32, (N, N), 0)
    lane_id = lax.broadcasted_iota(jnp.int32, (N, N), 1)
    places = []
    for side in range(2):
        coords = own_ref[...] if side == 0 else their_ref[...]
        for k in range(CAP):
            row, block, shift = corner(coords, k, p if side == 0 else before)
            keep = row_id >= row if side == 0 else row_id < row
            base = pl.multiple_of(block * N, N)
            near = pl.ds(base, N)
            far = pl.ds(pl.multiple_of(base + N, N), N)
            places.append((keep, near, far, shift))
    stores = []
    for part in range(2):
        total[part] = jnp.zeros((N, NCOL), f32)
        for tile_id, (keep, near, far, shift) in enumerate(places):
            tile = jnp.where(keep, grads_ref[tile_id, part].astype(f32), 0.0)
            total[part, :, near] += jnp.where(lane_id >= shift, tile, 0.0)
            total[part, :, far] += jnp.where(lane_id < shift, tile, 0.0)
        stores.append(pltpu.make_async_copy(total.at[part], out_ref.at[part, 0], sem.at[part]))
        stores[-1].start()
    for store in stores:
        store.wait()


def per_device(object_field, probe_wave, scan_coords, scan_counts, measured):
    vmem = pl.BlockSpec(memory_space=pltpu.VMEM)
    anywhere = pl.BlockSpec(memory_space=pl.ANY)
    hbm = pl.BlockSpec(memory_space=pltpu.HBM)
    dma = pltpu.SemaphoreType.DMA
    coords = scan_coords.T
    grads, theirs = pl.pallas_call(
        gather_kernel,
        out_shape=(
            pltpu.VMEM((2 * CAP, 2, N, N), bf16),
            pltpu.VMEM((2, CAP), jnp.int32),
        ),
        in_specs=[hbm, hbm, hbm, hbm, hbm, hbm],
        out_specs=(vmem, vmem),
        scratch_shapes=[
            pltpu.VMEM((2, CAP), jnp.int32),
            pltpu.SMEM((1,), jnp.int32),
            pltpu.VMEM((NCOL // N, 2, N, N), f32),
            pltpu.VMEM((2, N, N), f32),
            pltpu.VMEM((4, 2 * N, 2 * N), bf16),
            pltpu.VMEM((N, N), f32),
            pltpu.VMEM((8, N), f32),
            pltpu.VMEM((8, N), f32),
            pltpu.VMEM((2, CAP), jnp.int32),
            pltpu.VMEM((CAP, 2, N, N), bf16),
            pltpu.VMEM((CAP, 2, N, N), bf16),
            pltpu.VMEM((SLICES, 2, N, N), bf16),
            pltpu.VMEM((SLICES, 2, N, N), bf16),
            pltpu.VMEM((SLICES, 2, N, N), f32),
            pltpu.VMEM((SLICES, 2, N, N), bf16),
            dma((NCOL // N,)), dma((4,)), dma((2,)), dma((2,)), dma((2,)),
            dma((CAP,)), dma((SLICES,)), dma((CAP,)), dma((SLICES,)),
            dma((SLICES, 2)), dma((2 * CAP,)), dma,
        ],
        compiler_params=pltpu.CompilerParams(
            collective_id=0, has_side_effects=True, vmem_limit_bytes=60 << 20
        ),
        name="chain",
    )(coords, scan_counts, object_field, probe_wave, measured, jnp.asarray(tables()))
    return pl.pallas_call(
        scatter_kernel,
        out_shape=jax.ShapeDtypeStruct(object_field.shape, f32),
        in_specs=[vmem, vmem, vmem],
        out_specs=anywhere,
        scratch_shapes=[pltpu.VMEM((2, N, NCOL), f32), dma((2,))],
        compiler_params=pltpu.CompilerParams(vmem_limit_bytes=40 << 20),
        name="scatter",
    )(coords, theirs, grads)


def solution(mesh):
    in_specs = (P(None, "slab", "pos", None), P(), P("pos", None), P("pos"), P("pos", None, None))
    out_specs = P(None, "slab", "pos", None)
    return jax.shard_map(
        per_device, mesh=mesh, in_specs=in_specs, out_specs=out_specs, check_vma=False
    )
```

```python
import jax
import jax.numpy as jnp
import numpy as np
from jax import lax
from jax.experimental import pallas as pl
from jax.experimental.pallas import tpu as pltpu
from jax.sharding import PartitionSpec as P

f32 = jnp.float32
bf16 = jnp.bfloat16
N = 128
SLICES = 8
CAP = 3
NCOL = 2048
WORKERS = (0, 2, 4)
ORDER = (2, 1, 0)
DIRECT = 7
MESH = pl.DeviceIdType.MESH


def split_bf16(values):
    high = np.asarray(values, np.float32).astype(jnp.bfloat16)
    low = (values - high.astype(np.float64)).astype(np.float32).astype(jnp.bfloat16)
    return high, low


def tables():
    j = np.arange(N)
    fourier = np.exp(-2j * np.pi * ((j[:, None] * j) % N) / N) / np.sqrt(N)
    centred = (j + N // 2) % N - N // 2
    phase = np.exp(-0.5j * centred * centred / N)
    step = fourier.conj() @ (phase[:, None] * fourier)
    out = []
    for matrix in (step, fourier):
        real_high, real_low = split_bf16(matrix.real)
        imag_high, imag_low = split_bf16(matrix.imag)
        out.append(np.block([[real_high, real_low], [imag_high, imag_low]]))
        out.append(np.block([[real_high, imag_high], [real_low, imag_low]]))
    return np.stack(out)


def sandwich(left, right, real, imag, sign):
    x = jnp.concatenate([real.astype(bf16), imag.astype(bf16)], axis=1)
    x = jnp.concatenate([x, x], axis=0)
    a = jnp.dot(left[:N], x, preferred_element_type=f32)
    b = jnp.dot(left[N:], x, preferred_element_type=f32)
    if sign > 0:
        real, imag = a[:, :N] - b[:, N:], a[:, N:] + b[:, :N]
    else:
        real, imag = a[:, :N] + b[:, N:], a[:, N:] - b[:, :N]
    real = real.astype(bf16)
    imag = imag.astype(bf16)
    a = jnp.dot(jnp.concatenate([real, real], axis=1), right, preferred_element_type=f32)
    b = jnp.dot(jnp.concatenate([imag, imag], axis=1), right, preferred_element_type=f32)
    if sign > 0:
        return a[:, :N] - b[:, N:], a[:, N:] + b[:, :N]
    return a[:, :N] + b[:, N:], b[:, :N] - a[:, N:]


def corner(coords, k, strip):
    row = coords[0, k] - strip * N
    col = coords[1, k]
    block = jnp.minimum(lax.shift_right_arithmetic(col, 7), NCOL // N - 2)
    return row, block, col - block * N


def gather_kernel(
    coords_hbm, counts_hbm, object_ref, probe_ref, measured_ref, tables_ref,
    grads_ref, info_ref,
    coords_ref, counts_ref, strip, probe, table, sample, live, live_in, coords_in,
    top_out, low_out, tops, lows, kept, grad_out,
    block_sem, load_sem, coord_sem, sample_sem, live_sem,
    top_send, top_recv, low_send, low_recv, grad_send, grad_recv, own_sem, relay_send,
):
    s = lax.axis_index("slab")
    p = lax.axis_index("pos")
    strips = lax.axis_size("pos")
    after = lax.rem(p + 1, strips)
    before = lax.rem(p + strips - 1, strips)
    is_worker = (s == WORKERS[0]) | (s == WORKERS[1]) | (s == WORKERS[2])
    slot = s // 2

    load_coords = pltpu.make_async_copy(coords_hbm, coords_ref, load_sem.at[2])
    load_counts = pltpu.make_async_copy(counts_hbm, counts_ref, load_sem.at[3])
    load_coords.start()
    barrier = pltpu.get_barrier_semaphore()

    def greet(where):
        pl.semaphore_signal(barrier, inc=1, device_id=where, device_id_type=MESH)

    for w in WORKERS:
        greet((w, after))

        @pl.when(s != w)
        def _():
            greet((w, p))

    @pl.when(is_worker)
    def _():
        for other in range(SLICES):
            greet((other, before))

            @pl.when(s != other)
            def _():
                greet((other, p))

    greet((s, after))
    greet((s, before))

    def load_block(c):
        columns = pl.ds(pl.multiple_of(c * N, N), N)
        return pltpu.make_async_copy(object_ref.at[:, 0, :, columns], strip.at[c], block_sem.at[c])

    def start_block(c, carry):
        load_block(c).start()
        return carry

    def wait_block(c, carry):
        load_block(c).wait()
        return carry

    lax.fori_loop(0, NCOL // N, start_block, 0)
    load_probe = pltpu.make_async_copy(probe_ref, probe, load_sem.at[0])
    load_table = pltpu.make_async_copy(tables_ref, table, load_sem.at[1])

    @pl.when(is_worker)
    def _():
        load_probe.start()
        load_table.start()
        load_counts.start()
        pl.semaphore_wait(barrier, 22)

    @pl.when(jnp.logical_not(is_worker))
    def _():
        pl.semaphore_wait(barrier, 8)

    def send(src, dst, send_sem, recv_sem, where):
        return pltpu.make_async_remote_copy(
            src_ref=src, dst_ref=dst, send_sem=send_sem, recv_sem=recv_sem,
            device_id=where, device_id_type=MESH,
        )

    coord_copy = send(coords_ref, coords_in, coord_sem.at[0], coord_sem.at[1], (s, after))
    load_coords.wait()
    coord_copy.start()

    def sample_copy(k):
        return send(measured_ref.at[k], sample, sample_sem.at[0], sample_sem.at[1], (s, after))

    live_copy = send(live, live_in, live_sem.at[0], live_sem.at[1], (s, after))
    row_id = lax.broadcasted_iota(jnp.int32, (N, N), 0)
    lane_id = lax.broadcasted_iota(jnp.int32, (N, N), 1)

    def cut(keep, block, shift, dst, k):
        near = strip[block]
        far = strip[block + 1]
        for part in range(2):
            tile = jnp.where(lane_id >= shift, near[part], far[part])
            if part == 0:
                tile = tile - 1.0
            dst[k, part] = jnp.where(keep, tile, 0.0).astype(bf16)

    lax.fori_loop(0, NCOL // N, wait_block, 0)
    own = coords_ref[...]
    for k in ORDER:
        w = WORKERS[k]
        row, block, shift = corner(own, k, p)
        cut(row_id >= row, block, shift, top_out, k)
        send(top_out.at[k], tops.at[s], top_send.at[k], top_recv.at[s], (w, after)).start()

    coord_copy.wait_recv()
    theirs = coords_in[...]
    info_ref[...] = theirs
    corners = [corner(theirs, k, before) for k in range(CAP)]
    for k in ORDER:
        w = WORKERS[k]
        row, block, shift = corners[k]
        cut(row_id < row, block, shift, low_out, k)

        @pl.when(s != w)
        def _():
            send(low_out.at[k], lows.at[s], low_send.at[k], low_recv.at[s], (w, p)).start()

        @pl.when(s == w)
        def _():
            lows[s] = low_out[k]

    @pl.when(is_worker)
    def _():
        load_counts.wait()

    for k, w in enumerate(WORKERS):

        @pl.when(s == w)
        def _():
            sample_copy(k).start()
            live[...] = jnp.clip(jnp.full((8, N), counts_ref[0] - k, jnp.int32), 0, 1).astype(f32)
            live_copy.start()

    @pl.when(is_worker)
    def _():
        load_probe.wait()
        load_table.wait()

        def patch(i):
            return (
                tops[i, 0].astype(f32) + lows[i, 0].astype(f32),
                tops[i, 1].astype(f32) + lows[i, 1].astype(f32),
            )

        def arrive(i):
            send(top_out.at[0], tops.at[i], top_send.at[0], top_recv.at[i], (s, after)).wait_recv()

            @pl.when(i != s)
            def _():
                send(low_out.at[0], lows.at[i], low_send.at[0], low_recv.at[i], (s, p)).wait_recv()

        def through(i, real, imag):
            kept[i, 0] = real
            kept[i, 1] = imag
            arrive(i)
            d_real, d_imag = patch(i)
            return (
                real + (real * d_real - imag * d_imag),
                imag + (real * d_imag + imag * d_real),
            )

        def forward(i, wave):
            return sandwich(table[0], table[1], *through(i, *wave), 1)

        row = jnp.where(slot == 0, corners[0][0], jnp.where(slot == 1, corners[1][0], corners[2][0]))
        shift = jnp.where(slot == 0, corners[0][2], jnp.where(slot == 1, corners[1][2], corners[2][2]))

        def turned(x):
            return pltpu.roll(pltpu.roll(x, lax.rem(shift, N), 1), row, 0)

        wave = lax.fori_loop(0, SLICES - 1, forward, (turned(probe[0]), turned(probe[1])))
        real, imag = sandwich(table[2], table[3], *through(SLICES - 1, *wave), 1)
        sample_copy(0).wait_recv()
        live_copy.wait_recv()
        weight = (real * real + imag * imag - sample[...]) * live_in[0:1, :]
        moved = sandwich(table[2], table[3], weight * real, weight * imag, -1)

        def emit(i, moved):
            real, imag = moved
            grad_out[i, 0] = (kept[i, 0] * real + kept[i, 1] * imag).astype(bf16)
            grad_out[i, 1] = (kept[i, 0] * imag - kept[i, 1] * real).astype(bf16)

            @pl.when(i < DIRECT)
            def _():
                send(
                    grad_out.at[i], grads_ref.at[slot], grad_send.at[i, 0], grad_recv.at[slot],
                    (i, before),
                ).start()

            @pl.when(i != s)
            def _():
                send(
                    grad_out.at[i], grads_ref.at[CAP + slot], grad_send.at[i, 1],
                    grad_recv.at[CAP + slot], (i, p),
                ).start()

            @pl.when(i == s)
            def _():
                pltpu.make_async_copy(grad_out.at[i], grads_ref.at[CAP + slot], own_sem).start()

        def backward(step, moved):
            i = SLICES - 1 - step
            emit(i, moved)
            real, imag = moved
            d_real, d_imag = patch(i)
            return sandwich(
                table[0], table[1],
                real + (d_real * real + d_imag * imag),
                imag + (d_real * imag - d_imag * real),
                -1,
            )

        emit(0, lax.fori_loop(0, SLICES - 1, backward, moved))

    here = grad_out.at[0]

    def grad_wait(place):
        send(here, grads_ref.at[place], grad_send.at[0, 0], grad_recv.at[place], (s, after)).wait_recv()

    def relay(k):
        return send(
            grads_ref.at[CAP + k], grads_ref.at[k], relay_send.at[k], grad_recv.at[k], (s, before)
        )

    @pl.when(s >= DIRECT)
    def _():
        for k in ORDER:
            grad_wait(CAP + k)
            relay(k).start()

    for k, w in enumerate(WORKERS):
        grad_wait(k)

        @pl.when((s != w) & (s < DIRECT))
        def _():
            grad_wait(CAP + k)

        @pl.when(s != w)
        def _():
            send(low_out.at[k], lows.at[s], low_send.at[k], low_recv.at[s], (w, p)).wait_send()

        @pl.when(s == w)
        def _():
            pltpu.make_async_copy(here, grads_ref.at[CAP + k], own_sem).wait()
            sample_copy(k).wait_send()
            live_copy.wait_send()

        send(top_out.at[k], tops.at[s], top_send.at[k], top_recv.at[s], (w, after)).wait_send()

    @pl.when(s >= DIRECT)
    def _():
        for k in range(CAP):
            relay(k).wait_send()

    coord_copy.wait_send()

    @pl.when(is_worker)
    def _():
        def drain(i, carry):
            @pl.when(i < DIRECT)
            def _():
                send(
                    grad_out.at[i], grads_ref.at[slot], grad_send.at[i, 0], grad_recv.at[slot],
                    (i, before),
                ).wait_send()

            @pl.when(i != s)
            def _():
                send(
                    grad_out.at[i], grads_ref.at[CAP + slot], grad_send.at[i, 1],
                    grad_recv.at[CAP + slot], (i, p),
                ).wait_send()

            return carry

        lax.fori_loop(0, SLICES, drain, 0)


def scatter_kernel(own_ref, their_ref, grads_ref, out_ref, total, sem):
    p = lax.axis_index("pos")
    before = lax.rem(p + lax.axis_size("pos") - 1, lax.axis_size("pos"))
    row_id = lax.broadcasted_iota(jnp.int32, (N, N), 0)
    lane_id = lax.broadcasted_iota(jnp.int32, (N, N), 1)
    places = []
    for side in range(2):
        coords = own_ref[...] if side == 0 else their_ref[...]
        for k in range(CAP):
            row, block, shift = corner(coords, k, p if side == 0 else before)
            keep = row_id >= row if side == 0 else row_id < row
            base = pl.multiple_of(block * N, N)
            near = pl.ds(base, N)
            far = pl.ds(pl.multiple_of(base + N, N), N)
            places.append((keep, near, far, shift))
    stores = []
    for part in range(2):
        total[part] = jnp.zeros((N, NCOL), f32)
        for tile_id, (keep, near, far, shift) in enumerate(places):
            tile = jnp.where(keep, grads_ref[tile_id, part].astype(f32), 0.0)
            total[part, :, near] += jnp.where(lane_id >= shift, tile, 0.0)
            total[part, :, far] += jnp.where(lane_id < shift, tile, 0.0)
        stores.append(pltpu.make_async_copy(total.at[part], out_ref.at[part, 0], sem.at[part]))
        stores[-1].start()
    for store in stores:
        store.wait()


def per_device(object_field, probe_wave, scan_coords, scan_counts, measured):
    vmem = pl.BlockSpec(memory_space=pltpu.VMEM)
    anywhere = pl.BlockSpec(memory_space=pl.ANY)
    hbm = pl.BlockSpec(memory_space=pltpu.HBM)
    dma = pltpu.SemaphoreType.DMA
    coords = scan_coords.T
    grads, theirs = pl.pallas_call(
        gather_kernel,
        out_shape=(
            pltpu.VMEM((2 * CAP, 2, N, N), bf16),
            pltpu.VMEM((2, CAP), jnp.int32),
        ),
        in_specs=[hbm, hbm, hbm, hbm, hbm, hbm],
        out_specs=(vmem, vmem),
        scratch_shapes=[
            pltpu.VMEM((2, CAP), jnp.int32),
            pltpu.SMEM((1,), jnp.int32),
            pltpu.VMEM((NCOL // N, 2, N, N), f32),
            pltpu.VMEM((2, N, N), f32),
            pltpu.VMEM((4, 2 * N, 2 * N), bf16),
            pltpu.VMEM((N, N), f32),
            pltpu.VMEM((8, N), f32),
            pltpu.VMEM((8, N), f32),
            pltpu.VMEM((2, CAP), jnp.int32),
            pltpu.VMEM((CAP, 2, N, N), bf16),
            pltpu.VMEM((CAP, 2, N, N), bf16),
            pltpu.VMEM((SLICES, 2, N, N), bf16),
            pltpu.VMEM((SLICES, 2, N, N), bf16),
            pltpu.VMEM((SLICES, 2, N, N), f32),
            pltpu.VMEM((SLICES, 2, N, N), bf16),
            dma((NCOL // N,)), dma((4,)), dma((2,)), dma((2,)), dma((2,)),
            dma((CAP,)), dma((SLICES,)), dma((CAP,)), dma((SLICES,)),
            dma((SLICES, 2)), dma((2 * CAP,)), dma, dma((CAP,)),
        ],
        compiler_params=pltpu.CompilerParams(
            collective_id=0, has_side_effects=True, vmem_limit_bytes=60 << 20
        ),
        name="chain",
    )(coords, scan_counts, object_field, probe_wave, measured, jnp.asarray(tables()))
    return pl.pallas_call(
        scatter_kernel,
        out_shape=jax.ShapeDtypeStruct(object_field.shape, f32),
        in_specs=[vmem, vmem, vmem],
        out_specs=anywhere,
        scratch_shapes=[pltpu.VMEM((2, N, NCOL), f32), dma((2,))],
        compiler_params=pltpu.CompilerParams(vmem_limit_bytes=40 << 20),
        name="scatter",
    )(coords, theirs, grads)


def solution(mesh):
    in_specs = (P(None, "slab", "pos", None), P(), P("pos", None), P("pos"), P("pos", None, None))
    out_specs = P(None, "slab", "pos", None)
    return jax.shard_map(
        per_device, mesh=mesh, in_specs=in_specs, out_specs=out_specs, check_vma=False
    )
```

```python
import jax
import jax.numpy as jnp
import numpy as np
from jax import lax
from jax.experimental import pallas as pl
from jax.experimental.pallas import tpu as pltpu
from jax.sharding import PartitionSpec as P

f32 = jnp.float32
bf16 = jnp.bfloat16
N = 128
SLICES = 8
CAP = 3
NCOL = 2048
WORKERS = (0, 2, 4)
ORDER = (2, 1, 0)
DIRECT = 7
MESH = pl.DeviceIdType.MESH


def split_bf16(values):
    high = np.asarray(values, np.float32).astype(jnp.bfloat16)
    low = (values - high.astype(np.float64)).astype(np.float32).astype(jnp.bfloat16)
    return high, low


def tables():
    j = np.arange(N)
    fourier = np.exp(-2j * np.pi * ((j[:, None] * j) % N) / N) / np.sqrt(N)
    centred = (j + N // 2) % N - N // 2
    phase = np.exp(-0.5j * centred * centred / N)
    step = fourier.conj() @ (phase[:, None] * fourier)
    out = []
    for matrix in (step, fourier):
        real_high, real_low = split_bf16(matrix.real)
        imag_high, imag_low = split_bf16(matrix.imag)
        out.append(np.block([[real_high, real_low], [imag_high, imag_low]]))
        out.append(np.block([[real_high, imag_high], [real_low, imag_low]]))
    return np.stack(out)


def sandwich(left, right, real, imag, sign):
    x = jnp.concatenate([real.astype(bf16), imag.astype(bf16)], axis=1)
    x = jnp.concatenate([x, x], axis=0)
    a = jnp.dot(left[:N], x, preferred_element_type=f32)
    b = jnp.dot(left[N:], x, preferred_element_type=f32)
    if sign > 0:
        real, imag = a[:, :N] - b[:, N:], a[:, N:] + b[:, :N]
    else:
        real, imag = a[:, :N] + b[:, N:], a[:, N:] - b[:, :N]
    real = real.astype(bf16)
    imag = imag.astype(bf16)
    a = jnp.dot(jnp.concatenate([real, real], axis=1), right, preferred_element_type=f32)
    b = jnp.dot(jnp.concatenate([imag, imag], axis=1), right, preferred_element_type=f32)
    if sign > 0:
        return a[:, :N] - b[:, N:], a[:, N:] + b[:, :N]
    return a[:, :N] + b[:, N:], b[:, :N] - a[:, N:]


def corner(coords, k, strip):
    row = coords[0, k] - strip * N
    col = coords[1, k]
    block = jnp.minimum(lax.shift_right_arithmetic(col, 7), NCOL // N - 2)
    return row, block, col - block * N


def gather_kernel(
    coords_hbm, counts_hbm, object_ref, probe_ref, measured_ref, tables_ref,
    grads_ref, info_ref,
    coords_ref, counts_ref, strip, probe, table, sample, live, live_in, coords_in,
    top_out, low_out, tops, lows, kept, grad_out,
    block_sem, load_sem, coord_sem, sample_sem, live_sem,
    top_send, top_recv, low_send, low_recv, grad_send, grad_recv, own_sem, relay_send,
):
    s = lax.axis_index("slab")
    p = lax.axis_index("pos")
    strips = lax.axis_size("pos")
    after = lax.rem(p + 1, strips)
    before = lax.rem(p + strips - 1, strips)
    is_worker = (s == WORKERS[0]) | (s == WORKERS[1]) | (s == WORKERS[2])
    slot = s // 2

    load_coords = pltpu.make_async_copy(coords_hbm, coords_ref, load_sem.at[2])
    load_counts = pltpu.make_async_copy(counts_hbm, counts_ref, load_sem.at[3])
    load_coords.start()
    barrier = pltpu.get_barrier_semaphore()

    def greet(where):
        pl.semaphore_signal(barrier, inc=1, device_id=where, device_id_type=MESH)

    greet((s, before))

    @pl.when(is_worker)
    def _():
        for other in range(SLICES):
            greet((other, before))

            @pl.when(s != other)
            def _():
                greet((other, p))

    def load_block(c):
        columns = pl.ds(pl.multiple_of(c * N, N), N)
        return pltpu.make_async_copy(object_ref.at[:, 0, :, columns], strip.at[c], block_sem.at[c])

    def start_block(c, carry):
        load_block(c).start()
        return carry

    def wait_block(c, carry):
        load_block(c).wait()
        return carry

    lax.fori_loop(0, NCOL // N, start_block, 0)
    load_probe = pltpu.make_async_copy(probe_ref, probe, load_sem.at[0])
    load_table = pltpu.make_async_copy(tables_ref, table, load_sem.at[1])

    @pl.when(is_worker)
    def _():
        load_probe.start()
        load_table.start()
        load_counts.start()
        pl.semaphore_wait(barrier, 6)

    @pl.when(jnp.logical_not(is_worker))
    def _():
        pl.semaphore_wait(barrier, 7)

    def send(src, dst, send_sem, recv_sem, where):
        return pltpu.make_async_remote_copy(
            src_ref=src, dst_ref=dst, send_sem=send_sem, recv_sem=recv_sem,
            device_id=where, device_id_type=MESH,
        )

    coord_copy = send(coords_ref, coords_in, coord_sem.at[0], coord_sem.at[1], (s, after))
    load_coords.wait()
    coord_copy.start()

    def sample_copy(k):
        return send(measured_ref.at[k], sample, sample_sem.at[0], sample_sem.at[1], (s, after))

    live_copy = send(live, live_in, live_sem.at[0], live_sem.at[1], (s, after))
    row_id = lax.broadcasted_iota(jnp.int32, (N, N), 0)
    lane_id = lax.broadcasted_iota(jnp.int32, (N, N), 1)

    def cut(keep, block, shift, dst, k):
        near = strip[block]
        far = strip[block + 1]
        for part in range(2):
            tile = jnp.where(lane_id >= shift, near[part], far[part])
            if part == 0:
                tile = tile - 1.0
            dst[k, part] = jnp.where(keep, tile, 0.0).astype(bf16)

    lax.fori_loop(0, NCOL // N, wait_block, 0)
    own = coords_ref[...]
    for k in ORDER:
        w = WORKERS[k]
        row, block, shift = corner(own, k, p)
        cut(row_id >= row, block, shift, top_out, k)
        send(top_out.at[k], tops.at[s], top_send.at[k], top_recv.at[s], (w, after)).start()

    coord_copy.wait_recv()
    theirs = coords_in[...]
    info_ref[...] = theirs
    corners = [corner(theirs, k, before) for k in range(CAP)]
    for k in ORDER:
        w = WORKERS[k]
        row, block, shift = corners[k]
        cut(row_id < row, block, shift, low_out, k)

        @pl.when(s != w)
        def _():
            send(low_out.at[k], lows.at[s], low_send.at[k], low_recv.at[s], (w, p)).start()

        @pl.when(s == w)
        def _():
            lows[s] = low_out[k]

    @pl.when(is_worker)
    def _():
        load_counts.wait()

    for k, w in enumerate(WORKERS):

        @pl.when(s == w)
        def _():
            sample_copy(k).start()
            live[...] = jnp.clip(jnp.full((8, N), counts_ref[0] - k, jnp.int32), 0, 1).astype(f32)
            live_copy.start()

    @pl.when(is_worker)
    def _():
        load_probe.wait()
        load_table.wait()

        def patch(i):
            return (
                tops[i, 0].astype(f32) + lows[i, 0].astype(f32),
                tops[i, 1].astype(f32) + lows[i, 1].astype(f32),
            )

        def arrive(i):
            send(top_out.at[0], tops.at[i], top_send.at[0], top_recv.at[i], (s, after)).wait_recv()

            @pl.when(i != s)
            def _():
                send(low_out.at[0], lows.at[i], low_send.at[0], low_recv.at[i], (s, p)).wait_recv()

        def through(i, real, imag):
            kept[i, 0] = real
            kept[i, 1] = imag
            arrive(i)
            d_real, d_imag = patch(i)
            return (
                real + (real * d_real - imag * d_imag),
                imag + (real * d_imag + imag * d_real),
            )

        def forward(i, wave):
            return sandwich(table[0], table[1], *through(i, *wave), 1)

        row = jnp.where(slot == 0, corners[0][0], jnp.where(slot == 1, corners[1][0], corners[2][0]))
        shift = jnp.where(slot == 0, corners[0][2], jnp.where(slot == 1, corners[1][2], corners[2][2]))

        def turned(x):
            return pltpu.roll(pltpu.roll(x, lax.rem(shift, N), 1), row, 0)

        wave = lax.fori_loop(0, SLICES - 1, forward, (turned(probe[0]), turned(probe[1])))
        real, imag = sandwich(table[2], table[3], *through(SLICES - 1, *wave), 1)
        sample_copy(0).wait_recv()
        live_copy.wait_recv()
        weight = (real * real + imag * imag - sample[...]) * live_in[0:1, :]
        moved = sandwich(table[2], table[3], weight * real, weight * imag, -1)

        def emit(i, moved):
            real, imag = moved
            grad_out[i, 0] = (kept[i, 0] * real + kept[i, 1] * imag).astype(bf16)
            grad_out[i, 1] = (kept[i, 0] * imag - kept[i, 1] * real).astype(bf16)

            @pl.when(i < DIRECT)
            def _():
                send(
                    grad_out.at[i], grads_ref.at[slot], grad_send.at[i, 0], grad_recv.at[slot],
                    (i, before),
                ).start()

            @pl.when(i != s)
            def _():
                send(
                    grad_out.at[i], grads_ref.at[CAP + slot], grad_send.at[i, 1],
                    grad_recv.at[CAP + slot], (i, p),
                ).start()

            @pl.when(i == s)
            def _():
                pltpu.make_async_copy(grad_out.at[i], grads_ref.at[CAP + slot], own_sem).start()

        def backward(step, moved):
            i = SLICES - 1 - step
            emit(i, moved)
            real, imag = moved
            d_real, d_imag = patch(i)
            return sandwich(
                table[0], table[1],
                real + (d_real * real + d_imag * imag),
                imag + (d_real * imag - d_imag * real),
                -1,
            )

        emit(0, lax.fori_loop(0, SLICES - 1, backward, moved))

    here = grad_out.at[0]

    def grad_wait(place):
        send(here, grads_ref.at[place], grad_send.at[0, 0], grad_recv.at[place], (s, after)).wait_recv()

    def relay(k):
        return send(
            grads_ref.at[CAP + k], grads_ref.at[k], relay_send.at[k], grad_recv.at[k], (s, before)
        )

    @pl.when(s >= DIRECT)
    def _():
        for k in ORDER:
            grad_wait(CAP + k)
            relay(k).start()

    for k, w in enumerate(WORKERS):
        grad_wait(k)

        @pl.when((s != w) & (s < DIRECT))
        def _():
            grad_wait(CAP + k)

        @pl.when(s != w)
        def _():
            send(low_out.at[k], lows.at[s], low_send.at[k], low_recv.at[s], (w, p)).wait_send()

        @pl.when(s == w)
        def _():
            pltpu.make_async_copy(here, grads_ref.at[CAP + k], own_sem).wait()
            sample_copy(k).wait_send()
            live_copy.wait_send()

        send(top_out.at[k], tops.at[s], top_send.at[k], top_recv.at[s], (w, after)).wait_send()

    @pl.when(s >= DIRECT)
    def _():
        for k in range(CAP):
            relay(k).wait_send()

    coord_copy.wait_send()

    @pl.when(is_worker)
    def _():
        def drain(i, carry):
            @pl.when(i < DIRECT)
            def _():
                send(
                    grad_out.at[i], grads_ref.at[slot], grad_send.at[i, 0], grad_recv.at[slot],
                    (i, before),
                ).wait_send()

            @pl.when(i != s)
            def _():
                send(
                    grad_out.at[i], grads_ref.at[CAP + slot], grad_send.at[i, 1],
                    grad_recv.at[CAP + slot], (i, p),
                ).wait_send()

            return carry

        lax.fori_loop(0, SLICES, drain, 0)


def scatter_kernel(own_ref, their_ref, grads_ref, out_ref, total, sem):
    p = lax.axis_index("pos")
    before = lax.rem(p + lax.axis_size("pos") - 1, lax.axis_size("pos"))
    row_id = lax.broadcasted_iota(jnp.int32, (N, N), 0)
    lane_id = lax.broadcasted_iota(jnp.int32, (N, N), 1)
    places = []
    for side in range(2):
        coords = own_ref[...] if side == 0 else their_ref[...]
        for k in range(CAP):
            row, block, shift = corner(coords, k, p if side == 0 else before)
            keep = row_id >= row if side == 0 else row_id < row
            base = pl.multiple_of(block * N, N)
            near = pl.ds(base, N)
            far = pl.ds(pl.multiple_of(base + N, N), N)
            places.append((keep, near, far, shift))
    stores = []
    for part in range(2):
        total[part] = jnp.zeros((N, NCOL), f32)
        for tile_id, (keep, near, far, shift) in enumerate(places):
            tile = jnp.where(keep, grads_ref[tile_id, part].astype(f32), 0.0)
            total[part, :, near] += jnp.where(lane_id >= shift, tile, 0.0)
            total[part, :, far] += jnp.where(lane_id < shift, tile, 0.0)
        stores.append(pltpu.make_async_copy(total.at[part], out_ref.at[part, 0], sem.at[part]))
        stores[-1].start()
    for store in stores:
        store.wait()


def per_device(object_field, probe_wave, scan_coords, scan_counts, measured):
    vmem = pl.BlockSpec(memory_space=pltpu.VMEM)
    anywhere = pl.BlockSpec(memory_space=pl.ANY)
    hbm = pl.BlockSpec(memory_space=pltpu.HBM)
    dma = pltpu.SemaphoreType.DMA
    coords = scan_coords.T
    grads, theirs = pl.pallas_call(
        gather_kernel,
        out_shape=(
            pltpu.VMEM((2 * CAP, 2, N, N), bf16),
            pltpu.VMEM((2, CAP), jnp.int32),
        ),
        in_specs=[hbm, hbm, hbm, hbm, hbm, hbm],
        out_specs=(vmem, vmem),
        scratch_shapes=[
            pltpu.VMEM((2, CAP), jnp.int32),
            pltpu.SMEM((1,), jnp.int32),
            pltpu.VMEM((NCOL // N, 2, N, N), f32),
            pltpu.VMEM((2, N, N), f32),
            pltpu.VMEM((4, 2 * N, 2 * N), bf16),
            pltpu.VMEM((N, N), f32),
            pltpu.VMEM((8, N), f32),
            pltpu.VMEM((8, N), f32),
            pltpu.VMEM((2, CAP), jnp.int32),
            pltpu.VMEM((CAP, 2, N, N), bf16),
            pltpu.VMEM((CAP, 2, N, N), bf16),
            pltpu.VMEM((SLICES, 2, N, N), bf16),
            pltpu.VMEM((SLICES, 2, N, N), bf16),
            pltpu.VMEM((SLICES, 2, N, N), f32),
            pltpu.VMEM((SLICES, 2, N, N), bf16),
            dma((NCOL // N,)), dma((4,)), dma((2,)), dma((2,)), dma((2,)),
            dma((CAP,)), dma((SLICES,)), dma((CAP,)), dma((SLICES,)),
            dma((SLICES, 2)), dma((2 * CAP,)), dma, dma((CAP,)),
        ],
        compiler_params=pltpu.CompilerParams(
            collective_id=0, has_side_effects=True, vmem_limit_bytes=60 << 20
        ),
        name="chain",
    )(coords, scan_counts, object_field, probe_wave, measured, jnp.asarray(tables()))
    return pl.pallas_call(
        scatter_kernel,
        out_shape=jax.ShapeDtypeStruct(object_field.shape, f32),
        in_specs=[vmem, vmem, vmem],
        out_specs=anywhere,
        scratch_shapes=[pltpu.VMEM((2, N, NCOL), f32), dma((2,))],
        compiler_params=pltpu.CompilerParams(vmem_limit_bytes=40 << 20),
        name="scatter",
    )(coords, theirs, grads)


def solution(mesh):
    in_specs = (P(None, "slab", "pos", None), P(), P("pos", None), P("pos"), P("pos", None, None))
    out_specs = P(None, "slab", "pos", None)
    return jax.shard_map(
        per_device, mesh=mesh, in_specs=in_specs, out_specs=out_specs, check_vma=False
    )
```

```python
import jax
import jax.numpy as jnp
import numpy as np
from jax import lax
from jax.experimental import pallas as pl
from jax.experimental.pallas import tpu as pltpu
from jax.sharding import PartitionSpec as P

f32 = jnp.float32
bf16 = jnp.bfloat16
N = 128
SLICES = 8
CAP = 3
NCOL = 2048
WORKERS = (0, 3, 5)
ORDER = (2, 1, 0)
DIRECT = 7
MESH = pl.DeviceIdType.MESH


def split_bf16(values):
    high = np.asarray(values, np.float32).astype(jnp.bfloat16)
    low = (values - high.astype(np.float64)).astype(np.float32).astype(jnp.bfloat16)
    return high, low


def tables():
    j = np.arange(N)
    fourier = np.exp(-2j * np.pi * ((j[:, None] * j) % N) / N) / np.sqrt(N)
    centred = (j + N // 2) % N - N // 2
    phase = np.exp(-0.5j * centred * centred / N)
    step = fourier.conj() @ (phase[:, None] * fourier)
    out = []
    for matrix in (step, fourier):
        real_high, real_low = split_bf16(matrix.real)
        imag_high, imag_low = split_bf16(matrix.imag)
        out.append(np.block([[real_high, real_low], [imag_high, imag_low]]))
        out.append(np.block([[real_high, imag_high], [real_low, imag_low]]))
    return np.stack(out)


def sandwich(left, right, real, imag, sign):
    x = jnp.concatenate([real.astype(bf16), imag.astype(bf16)], axis=1)
    x = jnp.concatenate([x, x], axis=0)
    a = jnp.dot(left[:N], x, preferred_element_type=f32)
    b = jnp.dot(left[N:], x, preferred_element_type=f32)
    if sign > 0:
        real, imag = a[:, :N] - b[:, N:], a[:, N:] + b[:, :N]
    else:
        real, imag = a[:, :N] + b[:, N:], a[:, N:] - b[:, :N]
    real = real.astype(bf16)
    imag = imag.astype(bf16)
    a = jnp.dot(jnp.concatenate([real, real], axis=1), right, preferred_element_type=f32)
    b = jnp.dot(jnp.concatenate([imag, imag], axis=1), right, preferred_element_type=f32)
    if sign > 0:
        return a[:, :N] - b[:, N:], a[:, N:] + b[:, :N]
    return a[:, :N] + b[:, N:], b[:, :N] - a[:, N:]


def corner(coords, k, strip):
    row = coords[0, k] - strip * N
    col = coords[1, k]
    block = jnp.minimum(lax.shift_right_arithmetic(col, 7), NCOL // N - 2)
    return row, block, col - block * N


def gather_kernel(
    coords_hbm, counts_hbm, object_ref, probe_ref, measured_ref, tables_ref,
    grads_ref, info_ref,
    coords_ref, counts_ref, strip, probe, table, sample, live, live_in, coords_in,
    top_out, low_out, tops, lows, kept, grad_out,
    block_sem, load_sem, coord_sem, sample_sem, live_sem,
    top_send, top_recv, low_send, low_recv, grad_send, grad_recv, own_sem, relay_send,
):
    s = lax.axis_index("slab")
    p = lax.axis_index("pos")
    strips = lax.axis_size("pos")
    after = lax.rem(p + 1, strips)
    before = lax.rem(p + strips - 1, strips)
    is_worker = (s == WORKERS[0]) | (s == WORKERS[1]) | (s == WORKERS[2])
    slot = s // 2

    load_coords = pltpu.make_async_copy(coords_hbm, coords_ref, load_sem.at[2])
    load_counts = pltpu.make_async_copy(counts_hbm, counts_ref, load_sem.at[3])
    load_coords.start()
    barrier = pltpu.get_barrier_semaphore()

    def greet(where):
        pl.semaphore_signal(barrier, inc=1, device_id=where, device_id_type=MESH)

    greet((s, before))

    @pl.when(is_worker)
    def _():
        for other in range(SLICES):
            greet((other, before))

            @pl.when(s != other)
            def _():
                greet((other, p))

    def load_block(c):
        columns = pl.ds(pl.multiple_of(c * N, N), N)
        return pltpu.make_async_copy(object_ref.at[:, 0, :, columns], strip.at[c], block_sem.at[c])

    def start_block(c, carry):
        load_block(c).start()
        return carry

    def wait_block(c, carry):
        load_block(c).wait()
        return carry

    lax.fori_loop(0, NCOL // N, start_block, 0)
    load_probe = pltpu.make_async_copy(probe_ref, probe, load_sem.at[0])
    load_table = pltpu.make_async_copy(tables_ref, table, load_sem.at[1])

    @pl.when(is_worker)
    def _():
        load_probe.start()
        load_table.start()
        load_counts.start()
        pl.semaphore_wait(barrier, 6)

    @pl.when(jnp.logical_not(is_worker))
    def _():
        pl.semaphore_wait(barrier, 7)

    def send(src, dst, send_sem, recv_sem, where):
        return pltpu.make_async_remote_copy(
            src_ref=src, dst_ref=dst, send_sem=send_sem, recv_sem=recv_sem,
            device_id=where, device_id_type=MESH,
        )

    coord_copy = send(coords_ref, coords_in, coord_sem.at[0], coord_sem.at[1], (s, after))
    load_coords.wait()
    coord_copy.start()

    def sample_copy(k):
        return send(measured_ref.at[k], sample, sample_sem.at[0], sample_sem.at[1], (s, after))

    live_copy = send(live, live_in, live_sem.at[0], live_sem.at[1], (s, after))
    row_id = lax.broadcasted_iota(jnp.int32, (N, N), 0)
    lane_id = lax.broadcasted_iota(jnp.int32, (N, N), 1)

    def cut(keep, block, shift, dst, k):
        near = strip[block]
        far = strip[block + 1]
        for part in range(2):
            tile = jnp.where(lane_id >= shift, near[part], far[part])
            if part == 0:
                tile = tile - 1.0
            dst[k, part] = jnp.where(keep, tile, 0.0).astype(bf16)

    lax.fori_loop(0, NCOL // N, wait_block, 0)
    own = coords_ref[...]
    for k in ORDER:
        w = WORKERS[k]
        row, block, shift = corner(own, k, p)
        cut(row_id >= row, block, shift, top_out, k)
        send(top_out.at[k], tops.at[s], top_send.at[k], top_recv.at[s], (w, after)).start()

    coord_copy.wait_recv()
    theirs = coords_in[...]
    info_ref[...] = theirs
    corners = [corner(theirs, k, before) for k in range(CAP)]
    for k in ORDER:
        w = WORKERS[k]
        row, block, shift = corners[k]
        cut(row_id < row, block, shift, low_out, k)

        @pl.when(s != w)
        def _():
            send(low_out.at[k], lows.at[s], low_send.at[k], low_recv.at[s], (w, p)).start()

        @pl.when(s == w)
        def _():
            lows[s] = low_out[k]

    @pl.when(is_worker)
    def _():
        load_counts.wait()

    for k, w in enumerate(WORKERS):

        @pl.when(s == w)
        def _():
            sample_copy(k).start()
            live[...] = jnp.clip(jnp.full((8, N), counts_ref[0] - k, jnp.int32), 0, 1).astype(f32)
            live_copy.start()

    @pl.when(is_worker)
    def _():
        load_probe.wait()
        load_table.wait()

        def patch(i):
            return (
                tops[i, 0].astype(f32) + lows[i, 0].astype(f32),
                tops[i, 1].astype(f32) + lows[i, 1].astype(f32),
            )

        def arrive(i):
            send(top_out.at[0], tops.at[i], top_send.at[0], top_recv.at[i], (s, after)).wait_recv()

            @pl.when(i != s)
            def _():
                send(low_out.at[0], lows.at[i], low_send.at[0], low_recv.at[i], (s, p)).wait_recv()

        def through(i, real, imag):
            kept[i, 0] = real
            kept[i, 1] = imag
            arrive(i)
            d_real, d_imag = patch(i)
            return (
                real + (real * d_real - imag * d_imag),
                imag + (real * d_imag + imag * d_real),
            )

        def forward(i, wave):
            return sandwich(table[0], table[1], *through(i, *wave), 1)

        row = jnp.where(slot == 0, corners[0][0], jnp.where(slot == 1, corners[1][0], corners[2][0]))
        shift = jnp.where(slot == 0, corners[0][2], jnp.where(slot == 1, corners[1][2], corners[2][2]))

        def turned(x):
            return pltpu.roll(pltpu.roll(x, lax.rem(shift, N), 1), row, 0)

        wave = lax.fori_loop(0, SLICES - 1, forward, (turned(probe[0]), turned(probe[1])))
        real, imag = sandwich(table[2], table[3], *through(SLICES - 1, *wave), 1)
        sample_copy(0).wait_recv()
        live_copy.wait_recv()
        weight = (real * real + imag * imag - sample[...]) * live_in[0:1, :]
        moved = sandwich(table[2], table[3], weight * real, weight * imag, -1)

        def emit(i, moved):
            real, imag = moved
            grad_out[i, 0] = (kept[i, 0] * real + kept[i, 1] * imag).astype(bf16)
            grad_out[i, 1] = (kept[i, 0] * imag - kept[i, 1] * real).astype(bf16)

            @pl.when(i < DIRECT)
            def _():
                send(
                    grad_out.at[i], grads_ref.at[slot], grad_send.at[i, 0], grad_recv.at[slot],
                    (i, before),
                ).start()

            @pl.when(i != s)
            def _():
                send(
                    grad_out.at[i], grads_ref.at[CAP + slot], grad_send.at[i, 1],
                    grad_recv.at[CAP + slot], (i, p),
                ).start()

            @pl.when(i == s)
            def _():
                pltpu.make_async_copy(grad_out.at[i], grads_ref.at[CAP + slot], own_sem).start()

        def backward(step, moved):
            i = SLICES - 1 - step
            emit(i, moved)
            real, imag = moved
            d_real, d_imag = patch(i)
            return sandwich(
                table[0], table[1],
                real + (d_real * real + d_imag * imag),
                imag + (d_real * imag - d_imag * real),
                -1,
            )

        emit(0, lax.fori_loop(0, SLICES - 1, backward, moved))

    here = grad_out.at[0]

    def grad_wait(place):
        send(here, grads_ref.at[place], grad_send.at[0, 0], grad_recv.at[place], (s, after)).wait_recv()

    def relay(k):
        return send(
            grads_ref.at[CAP + k], grads_ref.at[k], relay_send.at[k], grad_recv.at[k], (s, before)
        )

    @pl.when(s >= DIRECT)
    def _():
        for k in ORDER:
            grad_wait(CAP + k)
            relay(k).start()

    for k, w in enumerate(WORKERS):
        grad_wait(k)

        @pl.when((s != w) & (s < DIRECT))
        def _():
            grad_wait(CAP + k)

        @pl.when(s != w)
        def _():
            send(low_out.at[k], lows.at[s], low_send.at[k], low_recv.at[s], (w, p)).wait_send()

        @pl.when(s == w)
        def _():
            pltpu.make_async_copy(here, grads_ref.at[CAP + k], own_sem).wait()
            sample_copy(k).wait_send()
            live_copy.wait_send()

        send(top_out.at[k], tops.at[s], top_send.at[k], top_recv.at[s], (w, after)).wait_send()

    @pl.when(s >= DIRECT)
    def _():
        for k in range(CAP):
            relay(k).wait_send()

    coord_copy.wait_send()

    @pl.when(is_worker)
    def _():
        def drain(i, carry):
            @pl.when(i < DIRECT)
            def _():
                send(
                    grad_out.at[i], grads_ref.at[slot], grad_send.at[i, 0], grad_recv.at[slot],
                    (i, before),
                ).wait_send()

            @pl.when(i != s)
            def _():
                send(
                    grad_out.at[i], grads_ref.at[CAP + slot], grad_send.at[i, 1],
                    grad_recv.at[CAP + slot], (i, p),
                ).wait_send()

            return carry

        lax.fori_loop(0, SLICES, drain, 0)


def scatter_kernel(own_ref, their_ref, grads_ref, out_ref, total, sem):
    p = lax.axis_index("pos")
    before = lax.rem(p + lax.axis_size("pos") - 1, lax.axis_size("pos"))
    row_id = lax.broadcasted_iota(jnp.int32, (N, N), 0)
    lane_id = lax.broadcasted_iota(jnp.int32, (N, N), 1)
    places = []
    for side in range(2):
        coords = own_ref[...] if side == 0 else their_ref[...]
        for k in range(CAP):
            row, block, shift = corner(coords, k, p if side == 0 else before)
            keep = row_id >= row if side == 0 else row_id < row
            base = pl.multiple_of(block * N, N)
            near = pl.ds(base, N)
            far = pl.ds(pl.multiple_of(base + N, N), N)
            places.append((keep, near, far, shift))
    stores = []
    for part in range(2):
        total[part] = jnp.zeros((N, NCOL), f32)
        for tile_id, (keep, near, far, shift) in enumerate(places):
            tile = jnp.where(keep, grads_ref[tile_id, part].astype(f32), 0.0)
            total[part, :, near] += jnp.where(lane_id >= shift, tile, 0.0)
            total[part, :, far] += jnp.where(lane_id < shift, tile, 0.0)
        stores.append(pltpu.make_async_copy(total.at[part], out_ref.at[part, 0], sem.at[part]))
        stores[-1].start()
    for store in stores:
        store.wait()


def per_device(object_field, probe_wave, scan_coords, scan_counts, measured):
    vmem = pl.BlockSpec(memory_space=pltpu.VMEM)
    anywhere = pl.BlockSpec(memory_space=pl.ANY)
    hbm = pl.BlockSpec(memory_space=pltpu.HBM)
    dma = pltpu.SemaphoreType.DMA
    coords = scan_coords.T
    grads, theirs = pl.pallas_call(
        gather_kernel,
        out_shape=(
            pltpu.VMEM((2 * CAP, 2, N, N), bf16),
            pltpu.VMEM((2, CAP), jnp.int32),
        ),
        in_specs=[hbm, hbm, hbm, hbm, hbm, hbm],
        out_specs=(vmem, vmem),
        scratch_shapes=[
            pltpu.VMEM((2, CAP), jnp.int32),
            pltpu.SMEM((1,), jnp.int32),
            pltpu.VMEM((NCOL // N, 2, N, N), f32),
            pltpu.VMEM((2, N, N), f32),
            pltpu.VMEM((4, 2 * N, 2 * N), bf16),
            pltpu.VMEM((N, N), f32),
            pltpu.VMEM((8, N), f32),
            pltpu.VMEM((8, N), f32),
            pltpu.VMEM((2, CAP), jnp.int32),
            pltpu.VMEM((CAP, 2, N, N), bf16),
            pltpu.VMEM((CAP, 2, N, N), bf16),
            pltpu.VMEM((SLICES, 2, N, N), bf16),
            pltpu.VMEM((SLICES, 2, N, N), bf16),
            pltpu.VMEM((SLICES, 2, N, N), f32),
            pltpu.VMEM((SLICES, 2, N, N), bf16),
            dma((NCOL // N,)), dma((4,)), dma((2,)), dma((2,)), dma((2,)),
            dma((CAP,)), dma((SLICES,)), dma((CAP,)), dma((SLICES,)),
            dma((SLICES, 2)), dma((2 * CAP,)), dma, dma((CAP,)),
        ],
        compiler_params=pltpu.CompilerParams(
            collective_id=0, has_side_effects=True, vmem_limit_bytes=60 << 20
        ),
        name="chain",
    )(coords, scan_counts, object_field, probe_wave, measured, jnp.asarray(tables()))
    return pl.pallas_call(
        scatter_kernel,
        out_shape=jax.ShapeDtypeStruct(object_field.shape, f32),
        in_specs=[vmem, vmem, vmem],
        out_specs=anywhere,
        scratch_shapes=[pltpu.VMEM((2, N, NCOL), f32), dma((2,))],
        compiler_params=pltpu.CompilerParams(vmem_limit_bytes=40 << 20),
        name="scatter",
    )(coords, theirs, grads)


def solution(mesh):
    in_specs = (P(None, "slab", "pos", None), P(), P("pos", None), P("pos"), P("pos", None, None))
    out_specs = P(None, "slab", "pos", None)
    return jax.shard_map(
        per_device, mesh=mesh, in_specs=in_specs, out_specs=out_specs, check_vma=False
    )
```

```python
import jax
import jax.numpy as jnp
import numpy as np
from jax import lax
from jax.experimental import pallas as pl
from jax.experimental.pallas import tpu as pltpu
from jax.sharding import PartitionSpec as P

f32 = jnp.float32
bf16 = jnp.bfloat16
N = 128
SLICES = 8
CAP = 3
NCOL = 2048
WORKERS = (0, 3, 7)
ORDER = (2, 1, 0)
RELAYED = 5
MESH = pl.DeviceIdType.MESH


def split_bf16(values):
    high = np.asarray(values, np.float32).astype(jnp.bfloat16)
    low = (values - high.astype(np.float64)).astype(np.float32).astype(jnp.bfloat16)
    return high, low


def tables():
    j = np.arange(N)
    fourier = np.exp(-2j * np.pi * ((j[:, None] * j) % N) / N) / np.sqrt(N)
    centred = (j + N // 2) % N - N // 2
    phase = np.exp(-0.5j * centred * centred / N)
    step = fourier.conj() @ (phase[:, None] * fourier)
    out = []
    for matrix in (step, fourier):
        real_high, real_low = split_bf16(matrix.real)
        imag_high, imag_low = split_bf16(matrix.imag)
        out.append(np.block([[real_high, real_low], [imag_high, imag_low]]))
        out.append(np.block([[real_high, imag_high], [real_low, imag_low]]))
    return np.stack(out)


def sandwich(left, right, real, imag, sign):
    x = jnp.concatenate([real.astype(bf16), imag.astype(bf16)], axis=1)
    x = jnp.concatenate([x, x], axis=0)
    a = jnp.dot(left[:N], x, preferred_element_type=f32)
    b = jnp.dot(left[N:], x, preferred_element_type=f32)
    if sign > 0:
        real, imag = a[:, :N] - b[:, N:], a[:, N:] + b[:, :N]
    else:
        real, imag = a[:, :N] + b[:, N:], a[:, N:] - b[:, :N]
    real = real.astype(bf16)
    imag = imag.astype(bf16)
    a = jnp.dot(jnp.concatenate([real, real], axis=1), right, preferred_element_type=f32)
    b = jnp.dot(jnp.concatenate([imag, imag], axis=1), right, preferred_element_type=f32)
    if sign > 0:
        return a[:, :N] - b[:, N:], a[:, N:] + b[:, :N]
    return a[:, :N] + b[:, N:], b[:, :N] - a[:, N:]


def corner(coords, k, strip):
    row = coords[0, k] - strip * N
    col = coords[1, k]
    block = jnp.minimum(lax.shift_right_arithmetic(col, 7), NCOL // N - 2)
    return row, block, col - block * N


def gather_kernel(
    coords_hbm, counts_hbm, object_ref, probe_ref, measured_ref, tables_ref,
    grads_ref, info_ref,
    coords_ref, counts_ref, strip, probe, table, sample, live, live_in, coords_in,
    top_out, low_out, tops, lows, kept, grad_out,
    block_sem, load_sem, coord_sem, sample_sem, live_sem,
    top_send, top_recv, low_send, low_recv, grad_send, grad_recv, own_sem, relay_send,
):
    s = lax.axis_index("slab")
    p = lax.axis_index("pos")
    strips = lax.axis_size("pos")
    after = lax.rem(p + 1, strips)
    before = lax.rem(p + strips - 1, strips)
    is_worker = (s == WORKERS[0]) | (s == WORKERS[1]) | (s == WORKERS[2])
    slot = s // 3

    load_coords = pltpu.make_async_copy(coords_hbm, coords_ref, load_sem.at[2])
    load_counts = pltpu.make_async_copy(counts_hbm, counts_ref, load_sem.at[3])
    load_coords.start()
    barrier = pltpu.get_barrier_semaphore()

    def greet(where):
        pl.semaphore_signal(barrier, inc=1, device_id=where, device_id_type=MESH)

    greet((s, before))

    @pl.when(is_worker)
    def _():
        for other in range(SLICES):
            greet((other, before))

            @pl.when(s != other)
            def _():
                greet((other, p))

    def load_block(c):
        columns = pl.ds(pl.multiple_of(c * N, N), N)
        return pltpu.make_async_copy(object_ref.at[:, 0, :, columns], strip.at[c], block_sem.at[c])

    def start_block(c, carry):
        load_block(c).start()
        return carry

    def wait_block(c, carry):
        load_block(c).wait()
        return carry

    lax.fori_loop(0, NCOL // N, start_block, 0)
    load_probe = pltpu.make_async_copy(probe_ref, probe, load_sem.at[0])
    load_table = pltpu.make_async_copy(tables_ref, table, load_sem.at[1])

    @pl.when(is_worker)
    def _():
        load_probe.start()
        load_table.start()
        load_counts.start()
        pl.semaphore_wait(barrier, 6)

    @pl.when(jnp.logical_not(is_worker))
    def _():
        pl.semaphore_wait(barrier, 7)

    def send(src, dst, send_sem, recv_sem, where):
        return pltpu.make_async_remote_copy(
            src_ref=src, dst_ref=dst, send_sem=send_sem, recv_sem=recv_sem,
            device_id=where, device_id_type=MESH,
        )

    coord_copy = send(coords_ref, coords_in, coord_sem.at[0], coord_sem.at[1], (s, after))
    load_coords.wait()
    coord_copy.start()

    def sample_copy(k):
        return send(measured_ref.at[k], sample, sample_sem.at[0], sample_sem.at[1], (s, after))

    live_copy = send(live, live_in, live_sem.at[0], live_sem.at[1], (s, after))
    row_id = lax.broadcasted_iota(jnp.int32, (N, N), 0)
    lane_id = lax.broadcasted_iota(jnp.int32, (N, N), 1)

    def cut(keep, block, shift, dst, k):
        near = strip[block]
        far = strip[block + 1]
        for part in range(2):
            tile = jnp.where(lane_id >= shift, near[part], far[part])
            if part == 0:
                tile = tile - 1.0
            dst[k, part] = jnp.where(keep, tile, 0.0).astype(bf16)

    lax.fori_loop(0, NCOL // N, wait_block, 0)
    own = coords_ref[...]
    for k in ORDER:
        w = WORKERS[k]
        row, block, shift = corner(own, k, p)
        cut(row_id >= row, block, shift, top_out, k)
        send(top_out.at[k], tops.at[s], top_send.at[k], top_recv.at[s], (w, after)).start()

    coord_copy.wait_recv()
    theirs = coords_in[...]
    info_ref[...] = theirs
    corners = [corner(theirs, k, before) for k in range(CAP)]
    for k in ORDER:
        w = WORKERS[k]
        row, block, shift = corners[k]
        cut(row_id < row, block, shift, low_out, k)

        @pl.when(s != w)
        def _():
            send(low_out.at[k], lows.at[s], low_send.at[k], low_recv.at[s], (w, p)).start()

        @pl.when(s == w)
        def _():
            lows[s] = low_out[k]

    @pl.when(is_worker)
    def _():
        load_counts.wait()

    for k, w in enumerate(WORKERS):

        @pl.when(s == w)
        def _():
            sample_copy(k).start()
            live[...] = jnp.clip(jnp.full((8, N), counts_ref[0] - k, jnp.int32), 0, 1).astype(f32)
            live_copy.start()

    @pl.when(is_worker)
    def _():
        load_probe.wait()
        load_table.wait()

        def patch(i):
            return (
                tops[i, 0].astype(f32) + lows[i, 0].astype(f32),
                tops[i, 1].astype(f32) + lows[i, 1].astype(f32),
            )

        def arrive(i):
            send(top_out.at[0], tops.at[i], top_send.at[0], top_recv.at[i], (s, after)).wait_recv()

            @pl.when(i != s)
            def _():
                send(low_out.at[0], lows.at[i], low_send.at[0], low_recv.at[i], (s, p)).wait_recv()

        def through(i, real, imag):
            kept[i, 0] = real
            kept[i, 1] = imag
            arrive(i)
            d_real, d_imag = patch(i)
            return (
                real + (real * d_real - imag * d_imag),
                imag + (real * d_imag + imag * d_real),
            )

        def forward(i, wave):
            return sandwich(table[0], table[1], *through(i, *wave), 1)

        row = jnp.where(slot == 0, corners[0][0], jnp.where(slot == 1, corners[1][0], corners[2][0]))
        shift = jnp.where(slot == 0, corners[0][2], jnp.where(slot == 1, corners[1][2], corners[2][2]))

        def turned(x):
            return pltpu.roll(pltpu.roll(x, lax.rem(shift, N), 1), row, 0)

        wave = lax.fori_loop(0, SLICES - 1, forward, (turned(probe[0]), turned(probe[1])))
        real, imag = sandwich(table[2], table[3], *through(SLICES - 1, *wave), 1)
        sample_copy(0).wait_recv()
        live_copy.wait_recv()
        weight = (real * real + imag * imag - sample[...]) * live_in[0:1, :]
        moved = sandwich(table[2], table[3], weight * real, weight * imag, -1)

        def emit(i, moved):
            real, imag = moved
            grad_out[i, 0] = (kept[i, 0] * real + kept[i, 1] * imag).astype(bf16)
            grad_out[i, 1] = (kept[i, 0] * imag - kept[i, 1] * real).astype(bf16)

            @pl.when(i != s)
            def _():
                send(
                    grad_out.at[i], grads_ref.at[CAP + slot], grad_send.at[i, 1],
                    grad_recv.at[CAP + slot], (i, p),
                ).start()

            @pl.when(i != RELAYED)
            def _():
                send(
                    grad_out.at[i], grads_ref.at[slot], grad_send.at[i, 0], grad_recv.at[slot],
                    (i, before),
                ).start()

            @pl.when(i == s)
            def _():
                pltpu.make_async_copy(grad_out.at[i], grads_ref.at[CAP + slot], own_sem).start()

        def backward(step, moved):
            i = SLICES - 1 - step
            emit(i, moved)
            real, imag = moved
            d_real, d_imag = patch(i)
            return sandwich(
                table[0], table[1],
                real + (d_real * real + d_imag * imag),
                imag + (d_real * imag - d_imag * real),
                -1,
            )

        emit(0, lax.fori_loop(0, SLICES - 1, backward, moved))

    here = grad_out.at[0]

    def grad_wait(place):
        send(here, grads_ref.at[place], grad_send.at[0, 0], grad_recv.at[place], (s, after)).wait_recv()

    def relay(k):
        return send(
            grads_ref.at[CAP + k], grads_ref.at[k], relay_send.at[k], grad_recv.at[k], (s, before)
        )

    @pl.when(s == RELAYED)
    def _():
        for k in ORDER:
            grad_wait(CAP + k)
            relay(k).start()

    for k, w in enumerate(WORKERS):
        grad_wait(k)

        @pl.when((s != w) & (s != RELAYED))
        def _():
            grad_wait(CAP + k)

        @pl.when(s != w)
        def _():
            send(low_out.at[k], lows.at[s], low_send.at[k], low_recv.at[s], (w, p)).wait_send()

        @pl.when(s == w)
        def _():
            pltpu.make_async_copy(here, grads_ref.at[CAP + k], own_sem).wait()
            sample_copy(k).wait_send()
            live_copy.wait_send()

        send(top_out.at[k], tops.at[s], top_send.at[k], top_recv.at[s], (w, after)).wait_send()

    @pl.when(s == RELAYED)
    def _():
        for k in range(CAP):
            relay(k).wait_send()

    coord_copy.wait_send()

    @pl.when(is_worker)
    def _():
        def drain(i, carry):
            @pl.when(i != RELAYED)
            def _():
                send(
                    grad_out.at[i], grads_ref.at[slot], grad_send.at[i, 0], grad_recv.at[slot],
                    (i, before),
                ).wait_send()

            @pl.when(i != s)
            def _():
                send(
                    grad_out.at[i], grads_ref.at[CAP + slot], grad_send.at[i, 1],
                    grad_recv.at[CAP + slot], (i, p),
                ).wait_send()

            return carry

        lax.fori_loop(0, SLICES, drain, 0)


def scatter_kernel(own_ref, their_ref, grads_ref, out_ref, total, sem):
    p = lax.axis_index("pos")
    before = lax.rem(p + lax.axis_size("pos") - 1, lax.axis_size("pos"))
    row_id = lax.broadcasted_iota(jnp.int32, (N, N), 0)
    lane_id = lax.broadcasted_iota(jnp.int32, (N, N), 1)
    places = []
    for side in range(2):
        coords = own_ref[...] if side == 0 else their_ref[...]
        for k in range(CAP):
            row, block, shift = corner(coords, k, p if side == 0 else before)
            keep = row_id >= row if side == 0 else row_id < row
            base = pl.multiple_of(block * N, N)
            near = pl.ds(base, N)
            far = pl.ds(pl.multiple_of(base + N, N), N)
            places.append((keep, near, far, shift))
    stores = []
    for part in range(2):
        total[part] = jnp.zeros((N, NCOL), f32)
        for tile_id, (keep, near, far, shift) in enumerate(places):
            tile = jnp.where(keep, grads_ref[tile_id, part].astype(f32), 0.0)
            total[part, :, near] += jnp.where(lane_id >= shift, tile, 0.0)
            total[part, :, far] += jnp.where(lane_id < shift, tile, 0.0)
        stores.append(pltpu.make_async_copy(total.at[part], out_ref.at[part, 0], sem.at[part]))
        stores[-1].start()
    for store in stores:
        store.wait()


def per_device(object_field, probe_wave, scan_coords, scan_counts, measured):
    vmem = pl.BlockSpec(memory_space=pltpu.VMEM)
    anywhere = pl.BlockSpec(memory_space=pl.ANY)
    hbm = pl.BlockSpec(memory_space=pltpu.HBM)
    dma = pltpu.SemaphoreType.DMA
    coords = scan_coords.T
    grads, theirs = pl.pallas_call(
        gather_kernel,
        out_shape=(
            pltpu.VMEM((2 * CAP, 2, N, N), bf16),
            pltpu.VMEM((2, CAP), jnp.int32),
        ),
        in_specs=[hbm, hbm, hbm, hbm, hbm, hbm],
        out_specs=(vmem, vmem),
        scratch_shapes=[
            pltpu.VMEM((2, CAP), jnp.int32),
            pltpu.SMEM((1,), jnp.int32),
            pltpu.VMEM((NCOL // N, 2, N, N), f32),
            pltpu.VMEM((2, N, N), f32),
            pltpu.VMEM((4, 2 * N, 2 * N), bf16),
            pltpu.VMEM((N, N), f32),
            pltpu.VMEM((8, N), f32),
            pltpu.VMEM((8, N), f32),
            pltpu.VMEM((2, CAP), jnp.int32),
            pltpu.VMEM((CAP, 2, N, N), bf16),
            pltpu.VMEM((CAP, 2, N, N), bf16),
            pltpu.VMEM((SLICES, 2, N, N), bf16),
            pltpu.VMEM((SLICES, 2, N, N), bf16),
            pltpu.VMEM((SLICES, 2, N, N), f32),
            pltpu.VMEM((SLICES, 2, N, N), bf16),
            dma((NCOL // N,)), dma((4,)), dma((2,)), dma((2,)), dma((2,)),
            dma((CAP,)), dma((SLICES,)), dma((CAP,)), dma((SLICES,)),
            dma((SLICES, 2)), dma((2 * CAP,)), dma, dma((CAP,)),
        ],
        compiler_params=pltpu.CompilerParams(
            collective_id=0, has_side_effects=True, vmem_limit_bytes=60 << 20
        ),
        name="chain",
    )(coords, scan_counts, object_field, probe_wave, measured, jnp.asarray(tables()))
    return pl.pallas_call(
        scatter_kernel,
        out_shape=jax.ShapeDtypeStruct(object_field.shape, f32),
        in_specs=[vmem, vmem, vmem],
        out_specs=anywhere,
        scratch_shapes=[pltpu.VMEM((2, N, NCOL), f32), dma((2,))],
        compiler_params=pltpu.CompilerParams(vmem_limit_bytes=40 << 20),
        name="scatter",
    )(coords, theirs, grads)


def solution(mesh):
    in_specs = (P(None, "slab", "pos", None), P(), P("pos", None), P("pos"), P("pos", None, None))
    out_specs = P(None, "slab", "pos", None)
    return jax.shard_map(
        per_device, mesh=mesh, in_specs=in_specs, out_specs=out_specs, check_vma=False
    )
```
